256 devices in a mesh: row: 64 (over z, y, x_hi), col: 4 (over x_lo, core).
Axes of the slice: x: 4 (x_hi: 2, x_lo: 2; x = x_hi * 2 + x_lo), y: 4, z: 8, core: 2. Of those that a mesh axis runs over, the one named last changes fastest.
Arguments:
- pair_rep: float32 [384, 384, 128], P('row', 'col'), may hold values from -6 to 6
- proj_weights: bfloat16 [2, 4, 128, 128], replicated, may hold values from -0.5 to 0.5
- gate_weights: bfloat16 [2, 128, 128], replicated, may hold values from -0.5 to 0.5
- out_weights: bfloat16 [2, 128, 128], replicated, may hold values from -0.5 to 0.5
Outputs:
- pair_out: float32 [384, 384, 128], P('row', 'col')
The draws below stay inside these ranges and needn't reach their ends.
All inputs are finite; a program needn't handle non-finite values.
Results may differ from the reference program's by a relative error of at most 0.013.
Values may be sent and summed in bfloat16 or wider, within the bound.
A program may use at most 128 MiB of HBM per device.

```python
import jax
import jax.numpy as jnp
from jax import lax

C = 128
HID = 128
N = 384


def block_scale(rng, extent, cuts, smallest, high):
    level, own = 1.0, jax.random.fold_in(rng, 6)
    for dim, parts in cuts:
        heights = jnp.exp(jax.random.uniform(jax.random.fold_in(own, dim), (parts,), jnp.float32, smallest / len(cuts), high / len(cuts)))
        level = level * jnp.repeat(heights, extent[dim] // parts).reshape([-1 if axis == dim else 1 for axis in range(len(extent))])
    return level


def gaussian(own_key, extent, width, reach, shards=(), dtype=jnp.bfloat16):
    entries = jax.random.normal(own_key, extent, jnp.float32) * width
    if len(shards) > 0:
        entries = block_scale(own_key, extent, shards, -0.22, 0.18) * entries
    return jnp.clip(entries, min=-reach, max=reach).astype(dtype)


def setup_inputs(seed: int = 0) -> dict:
    seeds = jax.random.split(jax.random.key(seed), 5)
    pair_rep = gaussian(seeds[0], (N, N, C), 1.0, 6.0, ((0, 64), (1, 4)), jnp.float32)
    proj_weights = gaussian(seeds[1], (2, 4, C, HID), C ** -0.5, 0.5)
    gate_weights = gaussian(seeds[2], (2, C, C), C ** -0.5, 0.5)
    out_weights = gaussian(seeds[3], (2, HID, C), HID ** -0.5, 0.5)
    return {"pair_rep": pair_rep, "proj_weights": proj_weights, "gate_weights": gate_weights, "out_weights": out_weights}


def normed(values):
    centred = values - lax.optimization_barrier(jnp.mean(values, axis=-1, keepdims=True))
    variance = lax.optimization_barrier(jnp.mean(centred * centred, axis=-1, keepdims=True))
    return centred * lax.rsqrt(variance + 1e-05)

def update(pair_block, proj_weights, gate_weights, out_weights, layer_index, outgoing):
    side_a, side_b, channels = pair_block.shape
    flat_norm = normed(pair_block).astype(jnp.bfloat16).reshape(side_a * side_b, channels)

    def linear(matrix):
        return jnp.dot(flat_norm, matrix, preferred_element_type=jnp.float32).reshape(side_a, side_b, matrix.shape[1])
    left_edge = (jax.nn.sigmoid(linear(proj_weights[layer_index, 0])) * linear(proj_weights[layer_index, 1])).astype(jnp.bfloat16)
    right_edge = (jax.nn.sigmoid(linear(proj_weights[layer_index, 2])) * linear(proj_weights[layer_index, 3])).astype(jnp.bfloat16)
    if outgoing:
        triangle = jnp.einsum('ikc,jkc->ijc', left_edge.astype(jnp.float32), right_edge.astype(jnp.float32), precision=lax.Precision.HIGHEST)
    else:
        triangle = jnp.einsum('kic,kjc->ijc', left_edge.astype(jnp.float32), right_edge.astype(jnp.float32), precision=lax.Precision.HIGHEST)
    tri_norm = normed(triangle).astype(jnp.bfloat16).reshape(side_a * side_b, -1)
    projected = jnp.dot(tri_norm, out_weights[layer_index], preferred_element_type=jnp.float32).reshape(side_a, side_b, channels)
    return pair_block + jax.nn.sigmoid(linear(gate_weights[layer_index])) * projected

def reference(pair_rep, proj_weights, gate_weights, out_weights):
    first = update(pair_rep, proj_weights, gate_weights, out_weights, 0, True)
    return update(first, proj_weights, gate_weights, out_weights, 1, False)
```

```python
import jax
import jax.numpy as jnp
from jax import lax
from jax.sharding import PartitionSpec as P


def normed(values):
    centred = values - jnp.mean(values, axis=-1, keepdims=True)
    variance = jnp.mean(centred * centred, axis=-1, keepdims=True)
    return centred * lax.rsqrt(variance + 1e-05)


def triangle(left_edge, right_edge, outgoing, rows):
    a, b, channels = left_edge.shape
    per = channels // rows
    edges = jnp.stack([left_edge, right_edge]).transpose(3, 0, 1, 2).reshape(rows, per, 2, a, b)
    edges = lax.all_to_all(edges, "row", split_axis=0, concat_axis=0, tiled=True)
    edges = edges.transpose(1, 2, 0, 3, 4).reshape(per, 2, rows * a, b)
    left, right = edges[:, 0], edges[:, 1]
    if outgoing:
        left = lax.all_gather(left, "col", axis=2, tiled=True)
        right = lax.all_to_all(right, "col", split_axis=1, concat_axis=2, tiled=True)
        tri = jnp.einsum("cik,cjk->cij", left, right, preferred_element_type=jnp.float32)
    else:
        left = lax.all_gather(left, "col", axis=2, tiled=True)
        tri = jnp.einsum("cki,ckj->cij", left, right, preferred_element_type=jnp.float32)
    tri = tri.astype(jnp.bfloat16).reshape(per, rows, a, b).transpose(1, 0, 2, 3)
    tri = lax.all_to_all(tri, "row", split_axis=0, concat_axis=0, tiled=True)
    return tri.reshape(channels, a, b).transpose(1, 2, 0).astype(jnp.float32)


def update(pair_block, proj_weights, gate_weights, out_weights, layer_index, outgoing, rows):
    side_a, side_b, channels = pair_block.shape
    flat_norm = normed(pair_block).astype(jnp.bfloat16).reshape(side_a * side_b, channels)

    def linear(matrix):
        return jnp.dot(flat_norm, matrix, preferred_element_type=jnp.float32).reshape(
            side_a, side_b, matrix.shape[1]
        )

    left_edge = (
        jax.nn.sigmoid(linear(proj_weights[layer_index, 0])) * linear(proj_weights[layer_index, 1])
    ).astype(jnp.bfloat16)
    right_edge = (
        jax.nn.sigmoid(linear(proj_weights[layer_index, 2])) * linear(proj_weights[layer_index, 3])
    ).astype(jnp.bfloat16)
    tri = triangle(left_edge, right_edge, outgoing, rows)
    tri_norm = normed(tri).astype(jnp.bfloat16).reshape(side_a * side_b, -1)
    projected = jnp.dot(
        tri_norm, out_weights[layer_index], preferred_element_type=jnp.float32
    ).reshape(side_a, side_b, channels)
    return pair_block + jax.nn.sigmoid(linear(gate_weights[layer_index])) * projected


def solution(mesh):
    rows = mesh.shape["row"]

    def per_device(pair_rep, proj_weights, gate_weights, out_weights):
        first = update(pair_rep, proj_weights, gate_weights, out_weights, 0, True, rows)
        return update(first, proj_weights, gate_weights, out_weights, 1, False, rows)

    return jax.shard_map(
        per_device,
        mesh=mesh,
        in_specs=(P("row", "col", None), P(), P(), P()),
        out_specs=P("row", "col", None),
        check_vma=False,
    )
```

```python
import jax
import jax.numpy as jnp
from jax import lax
from jax.experimental import pallas as pl
from jax.experimental.pallas import tpu as pltpu
from jax.sharding import PartitionSpec as P

MESH = pl.DeviceIdType.MESH
F32, BF16 = jnp.float32, jnp.bfloat16
Z, CHIPS, YX, XLO, CORES = 8, 16, 8, 2, 2
A, B, C = 6, 96, 128
GROUP = C // Z
POS, LANES = A * B, 640
ROWS = Z * A
NT = (((1,), (1,)), ((), ()))
TN = (((0,), (0,)), ((), ()))


def normed(values, axis):
    centred = values - jnp.mean(values, axis=axis, keepdims=True)
    variance = jnp.mean(centred * centred, axis=axis, keepdims=True)
    return centred * lax.rsqrt(variance + 1e-05)


def dot(a, b, dims=(((1,), (0,)), ((), ()))):
    return lax.dot_general(a, b, dims, preferred_element_type=F32)


def lane_of(rows):
    return lax.broadcasted_iota(jnp.int32, (rows, 128), 1)


def split_rows(tiles):
    lane = lane_of(tiles[0].shape[0])
    t0, t1, t2, t3, t4 = tiles
    pieces = [
        t0,
        pltpu.roll(jnp.where(lane < 64, t1, t0), 32, 1),
        pltpu.roll(jnp.where(lane < 32, t2, t1), 64, 1),
        pltpu.roll(t2, 96, 1),
        t3,
        pltpu.roll(jnp.where(lane < 64, t4, t3), 32, 1),
    ]
    return [jnp.where(lane < B, piece, 0.0) for piece in pieces]


def join_rows(pieces):
    lane = lane_of(pieces[0].shape[0])
    r0, r1, r2, r3, r4, r5 = pieces
    r1, r2, r3, r5 = (pltpu.roll(r, s, 1) for r, s in ((r1, 96), (r2, 64), (r3, 32), (r5, 96)))
    return [
        jnp.where(lane < 96, r0, r1),
        jnp.where(lane < 64, r1, r2),
        jnp.where(lane < 32, r2, r3),
        jnp.where(lane < 96, r4, r5),
        r5,
    ]


def picks_outgoing(core):
    row = lax.broadcasted_iota(jnp.int32, (XLO * 128, YX * ROWS), 0)
    col = lax.broadcasted_iota(jnp.int32, (XLO * 128, YX * ROWS), 1)
    x_lo, jr = row // 128, row % 128
    z = 4 * x_lo + 2 * core + jr // 48
    source = (jr % 48) // A * ROWS + z * A + jr % A
    return jnp.where((col == source) & (jr < B), 1.0, 0.0).astype(BF16)


def picks_incoming(core):
    row = lax.broadcasted_iota(jnp.int32, (YX * ROWS, 4 * 128), 0)
    col = lax.broadcasted_iota(jnp.int32, (YX * ROWS, 4 * 128), 1)
    yx, z, r = row // ROWS, row % ROWS // A, row % A
    other = jnp.bitwise_xor((z // 2) % 2, core)
    source = (other * 2 + z // 4) * 128 + (z % 2) * 48 + yx * A + r
    return jnp.where(col == source, 1.0, 0.0).astype(BF16)


def kernel(
    z_ref, proj_ref, gate_ref, out_ref, o_ref,
    sendz, recvz, spread, sendp, recvp, sendq, recvq, gather, sendx, recvx,
    zs, zr, ps, pr, cs, cr, qs, qr, xs, xr,
):
    row, col = lax.axis_index("row"), lax.axis_index("col")
    plane, yx, x_lo, core = row // YX, row % YX, col // CORES, col % CORES
    chip = yx * XLO + x_lo

    def on_plane(other_plane):
        return {"row": other_plane * YX + yx, "col": col}

    def on_chip(other_chip):
        return {"row": plane * YX + other_chip // XLO, "col": other_chip % XLO * CORES + core}

    other_core = {"row": row, "col": x_lo * CORES + 1 - core}

    barrier = pltpu.get_barrier_semaphore()
    peers = [on_plane((plane + s) % Z) for s in range(1, Z)]
    peers += [on_chip((chip + s) % CHIPS) for s in range(1, CHIPS)] + [other_core]
    for peer in peers:
        pl.semaphore_signal(barrier, inc=1, device_id=peer, device_id_type=MESH)

    def remote(src, dst, send, recv, peer):
        pltpu.make_async_remote_copy(
            src_ref=src, dst_ref=dst, send_sem=send, recv_sem=recv, device_id=peer, device_id_type=MESH
        ).start()

    def arrived(ref, sem):
        pltpu.make_async_copy(ref, ref, sem).wait()

    def slot_of(some_chip):
        return some_chip % XLO * YX + some_chip // XLO

    def over_planes(src, dst, send, recv):
        for s in range(1, Z):
            peer = (plane + s) % Z
            remote(src.at[peer], dst.at[plane], send, recv, on_plane(peer))
        pltpu.make_async_copy(src.at[plane], dst.at[plane], recv).start()

    def over_chips(src, dst, send, recv):
        for s in range(1, CHIPS):
            peer = (chip + s) % CHIPS
            remote(src.at[slot_of(peer)], dst.at[slot_of(chip)], send, recv, on_chip(peer))
        pltpu.make_async_copy(src.at[slot_of(chip)], dst.at[slot_of(chip)], recv).start()

    pair = z_ref[...].reshape(POS, C)
    for u in range(2):
        zn = normed(pair, -1).astype(BF16)
        for side in range(2):
            gated = dot(proj_ref[u, 2 * side].astype(F32).T.astype(BF16), zn, NT)
            value = dot(proj_ref[u, 2 * side + 1].astype(F32).T.astype(BF16), zn, NT)
            edge = (jax.nn.sigmoid(gated) * value).astype(BF16)
            sendz[u, side, :, :, 0:POS] = edge.reshape(Z, GROUP, POS)
            if u == 0 and side == 0:
                pl.semaphore_wait(barrier, len(peers))
            over_planes(sendz.at[u, side], recvz.at[u, side], zs.at[u, side], zr.at[u, side])
        gate = jax.nn.sigmoid(dot(zn, gate_ref[u]))
        picks = picks_outgoing(core) if u == 0 else picks_incoming(core)

        for side in range(2):
            arrived(recvz.at[u, side], zr.at[u, side])

            def spread_plane(p, carry, side=side, u=u):
                tiles = [recvz[u, side, p, :, t * 128 : t * 128 + 128].astype(F32) for t in range(5)]
                for r, piece in enumerate(split_rows(tiles)):
                    spread[u, side, pl.ds(p * A + r, GROUP, stride=ROWS), :] = piece
                return carry

            lax.fori_loop(0, Z, spread_plane, 0)
            for x in range(XLO):
                for c in range(YX):
                    at = (c * XLO + x) * ROWS
                    sendp[u, side, x * YX + c] = spread[u, side, at : at + ROWS, :].astype(BF16)
            over_chips(sendp.at[u, side], recvp.at[u, side, 0], ps.at[u, side], pr.at[u, side])

        for side in range(2):
            arrived(recvp.at[u, side, 0], pr.at[u, side])
            if u == 0 or side == 0:
                remote(recvp.at[u, side, 0], recvp.at[u, side, 1], cs.at[u, side], cr.at[u, side], other_core)

        def blocks(side, cores):
            return jnp.concatenate(
                [recvp[u, side, k, x * YX : x * YX + YX].reshape(YX * ROWS, 128) for k in range(cores) for x in range(XLO)], axis=1
            )

        arrived(recvp.at[u, 0, 1], cr.at[u, 0])
        if u == 0:
            arrived(recvp.at[u, 1, 1], cr.at[u, 1])
            right = dot(picks, blocks(1, 2)).astype(BF16)
            tri = dot(blocks(0, 2), right, NT)
        else:
            left = dot(picks, blocks(0, 2), NT).astype(BF16)
            tri = dot(left, blocks(1, 1))
        for x in range(XLO):
            sendq[u, x * YX : x * YX + YX] = tri[:, x * 128 : x * 128 + 128].astype(BF16).reshape(YX, ROWS, 128)
        over_chips(sendq.at[u], recvq.at[u], qs.at[u], qr.at[u])

        arrived(recvq.at[u], qr.at[u])
        for x in range(XLO):
            for c in range(YX):
                at = (c * XLO + x) * ROWS
                gather[u, at : at + ROWS, :] = recvq[u, x * YX + c].astype(F32)

        def gather_plane(p, carry, u=u):
            pieces = [gather[u, pl.ds(p * A + r, GROUP, stride=ROWS), :] for r in range(A)]
            for t, tile in enumerate(join_rows(pieces)):
                sendx[u, p, :, t * 128 : t * 128 + 128] = tile.astype(BF16)
            return carry

        lax.fori_loop(0, Z, gather_plane, 0)
        over_planes(sendx.at[u], recvx.at[u], xs.at[u], xr.at[u])
        arrived(recvx.at[u], xr.at[u])
        tri = recvx[u].reshape(C, LANES)[:, 0:POS].astype(F32)
        tn = normed(tri, 0).astype(BF16)
        pair = pair + gate * dot(tn, out_ref[u], TN)
    o_ref[...] = pair.reshape(A, B, C)

    for u in range(2):
        for side in range(2):
            arrived(recvz.at[u, side, pl.ds(0, Z - 1)], zs.at[u, side])
            arrived(recvp.at[u, side, 0, pl.ds(0, CHIPS - 1)], ps.at[u, side])
            if u == 0 or side == 0:
                arrived(recvp.at[u, side, 1], cs.at[u, side])
        arrived(recvq.at[u, pl.ds(0, CHIPS - 1)], qs.at[u])
        arrived(recvx.at[u, pl.ds(0, Z - 1)], xs.at[u])


def solution(mesh):
    vmem = pl.BlockSpec(memory_space=pltpu.VMEM)

    def per_device(pair_rep, proj_weights, gate_weights, out_weights):
        return pl.pallas_call(
            kernel,
            out_shape=jax.ShapeDtypeStruct(pair_rep.shape, pair_rep.dtype),
            in_specs=[vmem] * 4,
            out_specs=vmem,
            scratch_shapes=[
                pltpu.VMEM((2, 2, Z, GROUP, LANES), BF16),
                pltpu.VMEM((2, 2, Z, GROUP, LANES), BF16),
                pltpu.VMEM((2, 2, GROUP * ROWS, 128), F32),
                pltpu.VMEM((2, 2, CHIPS, ROWS, 128), BF16),
                pltpu.VMEM((2, 2, CORES, CHIPS, ROWS, 128), BF16),
                pltpu.VMEM((2, CHIPS, ROWS, 128), BF16),
                pltpu.VMEM((2, CHIPS, ROWS, 128), BF16),
                pltpu.VMEM((2, GROUP * ROWS, 128), F32),
                pltpu.VMEM((2, Z, GROUP, LANES), BF16),
                pltpu.VMEM((2, Z, GROUP, LANES), BF16),
            ]
            + [pltpu.SemaphoreType.DMA((2, 2))] * 6
            + [pltpu.SemaphoreType.DMA((2,))] * 4,
            compiler_params=pltpu.CompilerParams(
                collective_id=0, has_side_effects=True, vmem_limit_bytes=48 * 1024 * 1024
            ),
        )(pair_rep, proj_weights, gate_weights, out_weights)

    return jax.shard_map(
        per_device,
        mesh=mesh,
        in_specs=(P("row", "col", None), P(), P(), P()),
        out_specs=P("row", "col", None),
        check_vma=False,
    )
```

```python
import jax
import jax.numpy as jnp
from jax import lax
from jax.experimental import pallas as pl
from jax.experimental.pallas import tpu as pltpu
from jax.sharding import PartitionSpec as P

MESH = pl.DeviceIdType.MESH
F32, BF16 = jnp.float32, jnp.bfloat16
Z, CHIPS, YX, XLO, CORES = 8, 16, 8, 2, 2
A, B, C = 6, 96, 128
HALF = 8
POS, LANES = A * B, 640
ROWS = Z * A
FAR_PLANES = (4, 3, 5, 2, 6, 1, 7)
FAR_CHIPS = (10, 11, 9, 14, 6, 8, 2, 15, 13, 7, 5, 12, 4, 3, 1)
FAR_YX = (5, 7, 3, 4, 1, 6, 2, 0)
NT = (((1,), (1,)), ((), ()))
TN = (((0,), (0,)), ((), ()))


def normed(values, axis):
    centred = values - jnp.mean(values, axis=axis, keepdims=True)
    variance = jnp.mean(centred * centred, axis=axis, keepdims=True)
    return centred * lax.rsqrt(variance + 1e-05)


def dot(a, b, dims=(((1,), (0,)), ((), ()))):
    return lax.dot_general(a, b, dims, preferred_element_type=F32)


def lane_of(rows):
    return lax.broadcasted_iota(jnp.int32, (rows, 128), 1)


def split_rows(tiles):
    lane = lane_of(tiles[0].shape[0])
    t0, t1, t2, t3, t4 = tiles
    pieces = [
        t0,
        pltpu.roll(jnp.where(lane < 64, t1, t0), 32, 1),
        pltpu.roll(jnp.where(lane < 32, t2, t1), 64, 1),
        pltpu.roll(t2, 96, 1),
        t3,
        pltpu.roll(jnp.where(lane < 64, t4, t3), 32, 1),
    ]
    return [jnp.where(lane < B, piece, 0.0) for piece in pieces]


def picks_outgoing(core):
    row = lax.broadcasted_iota(jnp.int32, (XLO * 128, YX * ROWS), 0)
    col = lax.broadcasted_iota(jnp.int32, (XLO * 128, YX * ROWS), 1)
    x_lo, jr = row // 128, row % 128
    z = 4 * x_lo + 2 * core + jr // 48
    source = (jr % 48) // A * ROWS + z * A + jr % A
    return jnp.where((col == source) & (jr < B), 1.0, 0.0).astype(BF16)


def picks_incoming(core):
    row = lax.broadcasted_iota(jnp.int32, (YX * ROWS, 4 * 128), 0)
    col = lax.broadcasted_iota(jnp.int32, (YX * ROWS, 4 * 128), 1)
    yx, z, r = row // ROWS, row % ROWS // A, row % A
    other = jnp.bitwise_xor((z // 2) % 2, core)
    source = (other * 2 + z // 4) * 128 + (z % 2) * 48 + yx * A + r
    return jnp.where(col == source, 1.0, 0.0).astype(BF16)


def kernel(
    pair_hbm, proj_hbm, gate_hbm, out_hbm, o_ref,
    z_ref, proj_ref, gate_ref, out_ref, wide,
    sendz, recvz, spread, sendp, recvp, sendq, recvq, gather, sendx, recvx,
    load, zs, zr, ps, pr, cs, cr, qs, qr, xs, xr,
):
    loads = [
        pltpu.make_async_copy(src, dst, load.at[i])
        for i, (src, dst) in enumerate(
            ((pair_hbm, z_ref), (proj_hbm, proj_ref), (gate_hbm, gate_ref), (out_hbm, out_ref))
        )
    ]
    loads[0].start()
    loads[1].start()
    row, col = lax.axis_index("row"), lax.axis_index("col")
    plane, yx, x_lo, core = row >> 3, row & 7, col >> 1, col & 1
    chip = yx * XLO + x_lo
    chunk_of_chip = x_lo ^ ((yx >> 1) & 1)
    planes = [(plane + s) & (Z - 1) for s in FAR_PLANES]
    chips = [chip ^ s for s in FAR_CHIPS]

    def on_plane(other_plane):
        return {"row": other_plane * YX + yx, "col": col}

    def on_chip(other_chip):
        return {"row": plane * YX + (other_chip >> 1), "col": (other_chip & 1) * CORES + core}

    other_core = {"row": row, "col": col ^ 1}

    barrier = pltpu.get_barrier_semaphore()
    peers = [on_plane(peer) for peer in planes] + [on_chip(peer) for peer in chips] + [other_core]
    for peer in peers:
        pl.semaphore_signal(barrier, inc=1, device_id=peer, device_id_type=MESH)
    loads[2].start()
    loads[3].start()

    sent = []

    def remote(src, dst, send, recv, peer):
        pltpu.make_async_remote_copy(
            src_ref=src, dst_ref=dst, send_sem=send, recv_sem=recv, device_id=peer, device_id_type=MESH
        ).start()

    def arrived(ref, sem):
        pltpu.make_async_copy(ref, ref, sem).wait()

    def slot_of(some_chip):
        return (some_chip & 1) * YX + (some_chip >> 1)

    def over_planes(src, dst, send, recv):
        for peer in planes:
            remote(src.at[peer], dst.at[plane], send, recv, on_plane(peer))
        pltpu.make_async_copy(src.at[plane], dst.at[plane], recv).start()
        sent.append((src.at[pl.ds(0, Z - 1)], send))

    def to_owners(chunk, src, dst, send, recv):
        here = dst.at[slot_of(chip)]
        for s in FAR_YX[:-1]:
            peer = yx ^ s
            remote(src.at[peer], here, send, recv, on_chip(peer * XLO + (chunk ^ ((peer >> 1) & 1))))
        own = chunk_of_chip == chunk

        @pl.when(own)
        def _():
            pltpu.make_async_copy(src.at[yx], here, recv).start()

        @pl.when(jnp.logical_not(own))
        def _():
            remote(src.at[yx], here, send, recv, on_chip(chip ^ 1))

    def wide_weights(u):
        for i in range(4):
            turned = proj_ref[u, i].astype(F32).T.reshape(Z, 2, HALF, C)
            for k in range(2):
                wide[u, k, i] = turned[:, k].reshape(Z * HALF, C).astype(BF16)

    def update(u, pair):
        zn = normed(pair, -1).astype(BF16)
        for k in range(2):
            both = dot(wide[u, k].reshape(4 * Z * HALF, C), zn, NT).reshape(4, Z, HALF, POS)
            left = jax.nn.sigmoid(both[0]) * both[1]
            right = jax.nn.sigmoid(both[2]) * both[3]
            sendz[u, k, :, :, 0:POS] = jnp.concatenate([left, right], axis=1).astype(BF16)
            if u == 0 and k == 0:
                pl.semaphore_wait(barrier, len(peers))
            over_planes(sendz.at[u, k], recvz.at[u, k], zs.at[u, k], zr.at[u, k])
        if u == 0:
            wide_weights(1)
            loads[2].wait()
            loads[3].wait()
        gate = jax.nn.sigmoid(dot(zn, gate_ref[u]))
        picks = picks_outgoing(core) if u == 0 else picks_incoming(core)

        for k in range(2):
            arrived(recvz.at[u, k], zr.at[u, k])

            def spread_plane(p, carry):
                tiles = [recvz[u, k, p, :, t * 128 : t * 128 + 128].astype(F32) for t in range(5)]
                for r, piece in enumerate(split_rows(tiles)):
                    spread[u, k, pl.ds(p * A + r, 2 * HALF, stride=ROWS), :] = piece
                return carry

            lax.fori_loop(0, Z, spread_plane, 0, unroll=2)
            for side in range(2):
                for m in range(HALF):
                    at = (side * HALF + m) * ROWS
                    sendp[u, k, m, side] = spread[u, k, at : at + ROWS, :].astype(BF16)
            to_owners(k, sendp.at[u, k], recvp.at[u, 0], ps.at[u], pr.at[u])
        sent.append((recvp.at[u, 0, pl.ds(0, CHIPS - 1)], ps.at[u]))

        arrived(recvp.at[u, 0], pr.at[u])
        for side in range(2 if u == 0 else 1):
            src = recvp.at[u, 0, :, side]
            remote(src, recvp.at[u, 1, :, side], cs.at[u, side], cr.at[u, side], other_core)
            sent.append((src, cs.at[u, side]))
        for side in range(2 if u == 0 else 1):
            arrived(recvp.at[u, 1, :, side], cr.at[u, side])

        def blocks(side, cores):
            return jnp.concatenate(
                [
                    recvp[u, k, x * YX : x * YX + YX, side].reshape(YX * ROWS, 128)
                    for k in range(cores)
                    for x in range(XLO)
                ],
                axis=1,
            )

        if u == 0:
            right = dot(picks, blocks(1, 2)).astype(BF16)
            tri = dot(blocks(0, 2), right, NT)
        else:
            left = dot(picks, blocks(0, 2), NT).astype(BF16)
            tri = dot(left, blocks(1, 1))
        for x in range(XLO):
            sendq[u, x * YX : x * YX + YX] = tri[:, x * 128 : x * 128 + 128].astype(BF16).reshape(YX, ROWS, 128)
        here = recvq.at[u, chunk_of_chip, yx]
        for peer in chips:
            remote(sendq.at[u, slot_of(peer)], here, qs.at[u], qr.at[u, chunk_of_chip], on_chip(peer))
        pltpu.make_async_copy(sendq.at[u, slot_of(chip)], here, qr.at[u, chunk_of_chip]).start()
        sent.append((sendq.at[u, pl.ds(0, CHIPS - 1)], qs.at[u]))

        for k in range(2):
            arrived(recvq.at[u, k], qr.at[u, k])
            gather[u, k] = recvq[u, k].reshape(HALF * ROWS, 128).astype(F32)

            def gather_plane(p, carry):
                for r in range(0, A, 2):
                    pair_of_rows = [gather[u, k, pl.ds(p * A + r + i, HALF, stride=ROWS), :] for i in range(2)]
                    sendx[u, k, p, r * HALF : r * HALF + 2 * HALF] = jnp.concatenate(pair_of_rows, axis=0).astype(BF16)
                return carry

            lax.fori_loop(0, Z, gather_plane, 0, unroll=2)
            over_planes(sendx.at[u, k], recvx.at[u, k], xs.at[u, k], xr.at[u, k])
        for k in range(2):
            arrived(recvx.at[u, k], xr.at[u, k])
        tri = [recvx[u, k, p].astype(F32) for p in range(Z) for k in range(2)]
        for r in range(A):
            tri_row = jnp.concatenate([part[r * HALF : r * HALF + HALF] for part in tri], axis=0)
            projected = dot(normed(tri_row, 0).astype(BF16), out_ref[u], TN)[:B]
            rows = slice(r * B, r * B + B)
            o_ref[r] = pair[rows] + gate[rows] * projected

    loads[1].wait()
    wide_weights(0)
    loads[0].wait()
    update(0, z_ref[...].reshape(POS, C))
    update(1, o_ref[...].reshape(POS, C))
    for ref, sem in sent:
        arrived(ref, sem)


def solution(mesh):
    vmem = pl.BlockSpec(memory_space=pltpu.VMEM)

    def per_device(pair_rep, proj_weights, gate_weights, out_weights):
        return pl.pallas_call(
            kernel,
            out_shape=jax.ShapeDtypeStruct(pair_rep.shape, pair_rep.dtype),
            in_specs=[pl.BlockSpec(memory_space=pltpu.HBM)] * 4,
            out_specs=vmem,
            scratch_shapes=[
                pltpu.VMEM(pair_rep.shape, F32),
                pltpu.VMEM(proj_weights.shape, BF16),
                pltpu.VMEM(gate_weights.shape, BF16),
                pltpu.VMEM(out_weights.shape, BF16),
                pltpu.VMEM((2, 2, 4, Z * HALF, C), BF16),
                pltpu.VMEM((2, 2, Z, 2 * HALF, LANES), BF16),
                pltpu.VMEM((2, 2, Z, 2 * HALF, LANES), BF16),
                pltpu.VMEM((2, 2, 2 * HALF * ROWS, 128), F32),
                pltpu.VMEM((2, 2, HALF, 2, ROWS, 128), BF16),
                pltpu.VMEM((2, CORES, CHIPS, 2, ROWS, 128), BF16),
                pltpu.VMEM((2, CHIPS, ROWS, 128), BF16),
                pltpu.VMEM((2, 2, HALF, ROWS, 128), BF16),
                pltpu.VMEM((2, 2, HALF * ROWS, 128), F32),
                pltpu.VMEM((2, 2, Z, A * HALF, 128), BF16),
                pltpu.VMEM((2, 2, Z, A * HALF, 128), BF16),
                pltpu.SemaphoreType.DMA((4,)),
                pltpu.SemaphoreType.DMA((2, 2)),
                pltpu.SemaphoreType.DMA((2, 2)),
                pltpu.SemaphoreType.DMA((2,)),
                pltpu.SemaphoreType.DMA((2,)),
                pltpu.SemaphoreType.DMA((2, 2)),
                pltpu.SemaphoreType.DMA((2, 2)),
                pltpu.SemaphoreType.DMA((2,)),
                pltpu.SemaphoreType.DMA((2, 2)),
                pltpu.SemaphoreType.DMA((2, 2)),
                pltpu.SemaphoreType.DMA((2, 2)),
            ],
            compiler_params=pltpu.CompilerParams(
                collective_id=0, has_side_effects=True, vmem_limit_bytes=(65536 - 256) * 1024
            ),
        )(pair_rep, proj_weights, gate_weights, out_weights)

    return jax.shard_map(
        per_device,
        mesh=mesh,
        in_specs=(P("row", "col", None), P(), P(), P()),
        out_specs=P("row", "col", None),
        check_vma=False,
    )
```

```python
import jax
import jax.numpy as jnp
from jax import lax
from jax.experimental import pallas as pl
from jax.experimental.pallas import tpu as pltpu
from jax.sharding import PartitionSpec as P

MESH = pl.DeviceIdType.MESH
F32, BF16 = jnp.float32, jnp.bfloat16
Z, CHIPS, YX, XLO, CORES = 8, 16, 8, 2, 2
A, B, C = 6, 96, 128
HALF = 8
POS = A * B
ROWS = Z * A
FAR_PLANES = (4, 3, 5, 2, 6, 1, 7)
FAR_CHIPS = (10, 11, 9, 14, 6, 8, 2, 15, 13, 7, 5, 12, 4, 3, 1)
SIGNAL_ORDER = (0, 7, 1, 2, 8, 9, 10, 11, 3, 4, 12, 13, 14, 15, 16, 17, 5, 6, 18, 19, 20, 21, 22)
FAR_YX = (5, 7, 3, 4, 1, 6, 2, 0)
NT = (((1,), (1,)), ((), ()))
TN = (((0,), (0,)), ((), ()))


def normed(values, axis):
    centred = values - jnp.mean(values, axis=axis, keepdims=True)
    variance = jnp.mean(centred * centred, axis=axis, keepdims=True)
    return centred * lax.rsqrt(variance + 1e-05)


def dot(a, b, dims=(((1,), (0,)), ((), ()))):
    return lax.dot_general(a, b, dims, preferred_element_type=F32)


def lane_of(rows):
    return lax.broadcasted_iota(jnp.int32, (rows, 128), 1)


def rows_of_a(tiles):
    lane = lane_of(tiles[0].shape[0])
    t0, t1, t2 = tiles
    pieces = [
        t0,
        pltpu.roll(jnp.where(lane < 64, t1, t0), 32, 1),
        pltpu.roll(jnp.where(lane < 32, t2, t1), 64, 1),
        pltpu.roll(t2, 96, 1),
    ]
    return [jnp.where(lane < B, piece, 0.0) for piece in pieces]


def rows_of_b(tile, tail, tail_at):
    lane = lane_of(tile.shape[0])
    fifth = jnp.where(lane < 32, pltpu.roll(tile, 32, 1), pltpu.roll(tail, (32 - tail_at) % 128, 1))
    return [jnp.where(lane < B, piece, 0.0) for piece in (tile, fifth)]


def place(z, r, part):
    return z * 4 + r if part == 0 else 32 + z * 2 + r - 4


def picks_outgoing(core):
    row = lax.broadcasted_iota(jnp.int32, (XLO * 128, YX * ROWS), 0)
    col = lax.broadcasted_iota(jnp.int32, (XLO * 128, YX * ROWS), 1)
    x_lo, jr = row // 128, row % 128
    z, yx, r = 4 * x_lo + 2 * core + jr // 48, jr % 48 // A, jr % A
    source = jnp.where(r < 4, yx * 32 + z * 4 + r, 256 + yx * 16 + z * 2 + r - 4)
    return jnp.where((col == source) & (jr < B), 1.0, 0.0).astype(BF16)


def picks_incoming(core):
    row = lax.broadcasted_iota(jnp.int32, (YX * ROWS, 4 * 128), 0)
    col = lax.broadcasted_iota(jnp.int32, (YX * ROWS, 4 * 128), 1)
    in_a, late = row < 256, row - 256
    yx = jnp.where(in_a, row // 32, late // 16)
    z = jnp.where(in_a, row % 32 // 4, late % 16 // 2)
    r = jnp.where(in_a, row % 4, 4 + late % 2)
    other = jnp.bitwise_xor((z // 2) % 2, core)
    source = (other * 2 + z // 4) * 128 + (z % 2) * 48 + yx * A + r
    return jnp.where(col == source, 1.0, 0.0).astype(BF16)


def kernel(
    pair_hbm, proj_hbm, gate_hbm, out_hbm, o_ref,
    z_ref, proj_ref, gate_ref, out_ref, wide,
    senda, recva, send2, recv2, send1, recv1, spread, sendpa, sendpb, recvpa, recvpb, sendq, recvq, gather, sendx, recvx,
    load, zs, zr, ps, pr, cs, cr, qs, qr, xs, xr,
):
    loads = [
        pltpu.make_async_copy(src, dst, load.at[i])
        for i, (src, dst) in enumerate(
            ((pair_hbm, z_ref), (proj_hbm, proj_ref), (gate_hbm, gate_ref), (out_hbm, out_ref))
        )
    ]
    loads[0].start()
    loads[1].start()
    row, col = lax.axis_index("row"), lax.axis_index("col")
    plane, yx, x_lo, core = row >> 3, row & 7, col >> 1, col & 1
    chip = yx * XLO + x_lo
    chunk_of_chip = x_lo ^ ((yx >> 1) & 1)
    planes = [(plane + s) & (Z - 1) for s in FAR_PLANES]
    chips = [chip ^ s for s in FAR_CHIPS]

    def on_plane(other_plane):
        return {"row": other_plane * YX + yx, "col": col}

    def on_chip(other_chip):
        return {"row": plane * YX + (other_chip >> 1), "col": (other_chip & 1) * CORES + core}

    other_core = {"row": row, "col": col ^ 1}

    barrier = pltpu.get_barrier_semaphore()
    peers = [on_plane(peer) for peer in planes] + [on_chip(peer) for peer in chips] + [other_core]
    peers = [peers[i] for i in SIGNAL_ORDER]
    for peer in peers:
        pl.semaphore_signal(barrier, inc=1, device_id=peer, device_id_type=MESH)
    loads[2].start()
    loads[3].start()

    sent = []

    def remote(src, dst, send, recv, peer):
        pltpu.make_async_remote_copy(
            src_ref=src, dst_ref=dst, send_sem=send, recv_sem=recv, device_id=peer, device_id_type=MESH
        ).start()

    def arrived(ref, sem):
        pltpu.make_async_copy(ref, ref, sem).wait()

    def slot_of(some_chip):
        return (some_chip & 1) * YX + (some_chip >> 1)

    def over_planes(src, dst, send, recv):
        for peer in planes:
            remote(src.at[peer], dst.at[plane], send, recv, on_plane(peer))
        pltpu.make_async_copy(src.at[plane], dst.at[plane], recv).start()
        sent.append((src.at[pl.ds(0, Z - 1)], send))

    def to_owners(chunk, src, dst, send, recv):
        here = dst.at[slot_of(chip)]
        for s in FAR_YX[:-1]:
            peer = yx ^ s
            remote(src.at[peer], here, send, recv, on_chip(peer * XLO + (chunk ^ ((peer >> 1) & 1))))
        own = chunk_of_chip == chunk

        @pl.when(own)
        def _():
            pltpu.make_async_copy(src.at[yx], here, recv).start()

        @pl.when(jnp.logical_not(own))
        def _():
            remote(src.at[yx], here, send, recv, on_chip(chip ^ 1))

    def wide_weights(u):
        for i in range(4):
            turned = proj_ref[u, i].astype(F32).T.reshape(Z, 2, HALF, C)
            for k in range(2):
                wide[u, k, i] = turned[:, k].reshape(Z * HALF, C).astype(BF16)

    def update(u, pair):
        zn = normed(pair, -1).astype(BF16)

        def edges(k, some):
            both = dot(wide[u, k].reshape(4 * Z * HALF, C), some, NT).reshape(4, Z, HALF, some.shape[0])
            left = jax.nn.sigmoid(both[0]) * both[1]
            right = jax.nn.sigmoid(both[2]) * both[3]
            return jnp.concatenate([left, right], axis=1).astype(BF16)

        z_parts = [(senda.at[u, 0], recva.at[u, 0]), (send2.at[u], recv2.at[u])]
        z_parts += [(senda.at[u, 1], recva.at[u, 1]), (send1.at[u], recv1.at[u])]
        first = edges(0, zn)
        senda[u, 0] = first[:, :, 0:384]
        if u == 0:
            pl.semaphore_wait(barrier, len(peers))
        over_planes(*z_parts[0], zs.at[u, 0], zr.at[u, 0])
        send2[u, :, :, 0:192] = first[:, :, 384:POS]
        send2[u, :, :, 192:256] = edges(1, zn[512:POS])
        over_planes(*z_parts[1], zs.at[u, 1], zr.at[u, 1])
        second = edges(1, zn[0:512])
        senda[u, 1] = second[:, :, 0:384]
        send1[u] = second[:, :, 384:512]
        over_planes(*z_parts[2], zs.at[u, 2], zr.at[u, 2])
        over_planes(*z_parts[3], zs.at[u, 3], zr.at[u, 3])
        if u == 0:
            wide_weights(1)
            loads[2].wait()
            loads[3].wait()
        gate = jax.nn.sigmoid(dot(zn, gate_ref[u]))
        picks = picks_outgoing(core) if u == 0 else picks_incoming(core)

        for k in range(2):
            for part in range(2):
                arrived(z_parts[2 * k + part][1], zr.at[u, 2 * k + part])

                def spread_plane(p, carry):
                    if part == 0:
                        tiles = [recva[u, k, p, :, t * 128 : t * 128 + 128].astype(F32) for t in range(3)]
                        pieces = rows_of_a(tiles)
                    else:
                        tile = recv2[u, p, :, 0:128] if k == 0 else recv1[u, p]
                        pieces = rows_of_b(tile.astype(F32), recv2[u, p, :, 128:256].astype(F32), 64 * k)
                    for i, piece in enumerate(pieces):
                        spread[u, k, pl.ds(place(p, 4 * part + i, part), 2 * HALF, stride=ROWS), :] = piece
                    return carry

                lax.fori_loop(0, Z, spread_plane, 0, unroll=2)
                sendp, lo, hi = (sendpa, 0, 32) if part == 0 else (sendpb, 32, ROWS)
                for side in range(2):
                    for m in range(HALF):
                        at = (side * HALF + m) * ROWS
                        sendp[u, k, m, side] = spread[u, k, at + lo : at + hi, :].astype(BF16)
                recvp = (recvpa, recvpb)[part]
                to_owners(k, sendp.at[u, k], recvp.at[u, 0], ps.at[u, part], pr.at[u, part])

        sides = pl.ds(0, 2 if u == 0 else 1)
        for part, recvp in enumerate((recvpa, recvpb)):
            sent.append((recvp.at[u, 0, pl.ds(0, CHIPS - 1)], ps.at[u, part]))
            arrived(recvp.at[u, 0], pr.at[u, part])
            src = recvp.at[u, 0, :, sides]
            remote(src, recvp.at[u, 1, :, sides], cs.at[u, part], cr.at[u, part], other_core)
            sent.append((src, cs.at[u, part]))
        for part, recvp in enumerate((recvpa, recvpb)):
            arrived(recvp.at[u, 1, :, sides], cr.at[u, part])

        def blocks(side, cores):
            return jnp.concatenate(
                [
                    jnp.concatenate(
                        [
                            recvpa[u, k, x * YX : x * YX + YX, side].reshape(256, 128),
                            recvpb[u, k, x * YX : x * YX + YX, side].reshape(128, 128),
                        ],
                        axis=0,
                    )
                    for k in range(cores)
                    for x in range(XLO)
                ],
                axis=1,
            )

        if u == 0:
            right = dot(picks, blocks(1, 2)).astype(BF16)
            tri = dot(blocks(0, 2), right, NT)
        else:
            left = dot(picks, blocks(0, 2), NT).astype(BF16)
            tri = dot(left, blocks(1, 1))
        for x in range(XLO):
            block = tri[:, x * 128 : x * 128 + 128].astype(BF16)
            sendq[u, x * YX : x * YX + YX, 0:32] = block[0:256].reshape(YX, 32, 128)
            sendq[u, x * YX : x * YX + YX, 32:ROWS] = block[256:384].reshape(YX, 16, 128)
        here = recvq.at[u, chunk_of_chip, yx]
        for peer in chips:
            remote(sendq.at[u, slot_of(peer)], here, qs.at[u], qr.at[u, chunk_of_chip], on_chip(peer))
        pltpu.make_async_copy(sendq.at[u, slot_of(chip)], here, qr.at[u, chunk_of_chip]).start()
        sent.append((sendq.at[u, pl.ds(0, CHIPS - 1)], qs.at[u]))

        for k in range(2):
            arrived(recvq.at[u, k], qr.at[u, k])
            gather[u, k] = recvq[u, k].reshape(HALF * ROWS, 128).astype(F32)

            def gather_plane(p, carry):
                for r in range(0, A, 2):
                    pair_of_rows = [
                        gather[u, k, pl.ds(place(p, r + i, r // 4), HALF, stride=ROWS), :] for i in range(2)
                    ]
                    sendx[u, k, p, r * HALF : r * HALF + 2 * HALF] = jnp.concatenate(pair_of_rows, axis=0).astype(BF16)
                return carry

            lax.fori_loop(0, Z, gather_plane, 0, unroll=2)
            over_planes(sendx.at[u, k], recvx.at[u, k], xs.at[u, k], xr.at[u, k])
        for k in range(2):
            arrived(recvx.at[u, k], xr.at[u, k])
        tri = [recvx[u, k, p].astype(F32) for p in range(Z) for k in range(2)]
        for r in range(A):
            tri_row = jnp.concatenate([part[r * HALF : r * HALF + HALF] for part in tri], axis=0)
            projected = dot(normed(tri_row, 0).astype(BF16), out_ref[u], TN)[:B]
            rows = slice(r * B, r * B + B)
            o_ref[r] = pair[rows] + gate[rows] * projected

    loads[1].wait()
    wide_weights(0)
    loads[0].wait()
    update(0, z_ref[...].reshape(POS, C))
    update(1, o_ref[...].reshape(POS, C))
    for ref, sem in sent:
        arrived(ref, sem)


def solution(mesh):
    vmem = pl.BlockSpec(memory_space=pltpu.VMEM)

    def per_device(*operands):
        pair_rep, proj_weights, gate_weights, out_weights = operands
        return pl.pallas_call(
            kernel,
            out_shape=jax.ShapeDtypeStruct(pair_rep.shape, pair_rep.dtype),
            in_specs=[pl.BlockSpec(memory_space=pltpu.HBM)] * 4,
            out_specs=vmem,
            scratch_shapes=[
                pltpu.VMEM(pair_rep.shape, F32),
                pltpu.VMEM(proj_weights.shape, BF16),
                pltpu.VMEM(gate_weights.shape, BF16),
                pltpu.VMEM(out_weights.shape, BF16),
                pltpu.VMEM((2, 2, 4, Z * HALF, C), BF16),
                pltpu.VMEM((2, 2, Z, 2 * HALF, 384), BF16),
                pltpu.VMEM((2, 2, Z, 2 * HALF, 384), BF16),
                pltpu.VMEM((2, Z, 2 * HALF, 256), BF16),
                pltpu.VMEM((2, Z, 2 * HALF, 256), BF16),
                pltpu.VMEM((2, Z, 2 * HALF, 128), BF16),
                pltpu.VMEM((2, Z, 2 * HALF, 128), BF16),
                pltpu.VMEM((2, 2, 2 * HALF * ROWS, 128), F32),
                pltpu.VMEM((2, 2, HALF, 2, 32, 128), BF16),
                pltpu.VMEM((2, 2, HALF, 2, 16, 128), BF16),
                pltpu.VMEM((2, CORES, CHIPS, 2, 32, 128), BF16),
                pltpu.VMEM((2, CORES, CHIPS, 2, 16, 128), BF16),
                pltpu.VMEM((2, CHIPS, ROWS, 128), BF16),
                pltpu.VMEM((2, 2, HALF, ROWS, 128), BF16),
                pltpu.VMEM((2, 2, HALF * ROWS, 128), F32),
                pltpu.VMEM((2, 2, Z, A * HALF, 128), BF16),
                pltpu.VMEM((2, 2, Z, A * HALF, 128), BF16),
                pltpu.SemaphoreType.DMA((4,)),
                pltpu.SemaphoreType.DMA((2, 4)),
                pltpu.SemaphoreType.DMA((2, 4)),
                pltpu.SemaphoreType.DMA((2, 2)),
                pltpu.SemaphoreType.DMA((2, 2)),
                pltpu.SemaphoreType.DMA((2, 2)),
                pltpu.SemaphoreType.DMA((2, 2)),
                pltpu.SemaphoreType.DMA((2,)),
                pltpu.SemaphoreType.DMA((2, 2)),
                pltpu.SemaphoreType.DMA((2, 2)),
                pltpu.SemaphoreType.DMA((2, 2)),
            ],
            compiler_params=pltpu.CompilerParams(
                collective_id=0, has_side_effects=True, vmem_limit_bytes=48 * 1024 * 1024
            ),
        )(*(pltpu.with_memory_space_constraint(x, pltpu.HBM) for x in operands))

    return jax.shard_map(
        per_device,
        mesh=mesh,
        in_specs=(P("row", "col", None), P(), P(), P()),
        out_specs=P("row", "col", None),
        check_vma=False,
    )
```

```python
import jax
import jax.numpy as jnp
from jax import lax
from jax.experimental import pallas as pl
from jax.experimental.pallas import tpu as pltpu
from jax.sharding import PartitionSpec as P

MESH = pl.DeviceIdType.MESH
F32, BF16 = jnp.float32, jnp.bfloat16
Z, CHIPS, YX, XLO, CORES = 8, 16, 8, 2, 2
A, B, C = 6, 96, 128
HALF = 8
POS = A * B
ROWS = Z * A
FAR_PLANES = (4, 3, 5, 2, 6, 1, 7)
FAR_CHIPS = (10, 11, 9, 14, 6, 8, 2, 15, 13, 7, 5, 12, 4, 3, 1)
PLANE_HOPS = (4, 3, 3, 2, 2, 1, 1)
CHIP_HOPS = (4, 3, 3, 3, 3, 2, 2, 2, 2, 2, 2, 1, 1, 1, 1)
FAR_YX = (5, 7, 3, 4, 1, 6, 2, 0)
NT = (((1,), (1,)), ((), ()))
TN = (((0,), (0,)), ((), ()))


def normed(values, axis):
    centred = values - jnp.mean(values, axis=axis, keepdims=True)
    variance = jnp.mean(centred * centred, axis=axis, keepdims=True)
    return centred * lax.rsqrt(variance + 1e-05)


def dot(a, b, dims=(((1,), (0,)), ((), ()))):
    return lax.dot_general(a, b, dims, preferred_element_type=F32)


def lane_of(rows):
    return lax.broadcasted_iota(jnp.int32, (rows, 128), 1)


def rows_of_a(tiles):
    lane = lane_of(tiles[0].shape[0])
    t0, t1, t2 = tiles
    pieces = [
        t0,
        pltpu.roll(jnp.where(lane < 64, t1, t0), 32, 1),
        pltpu.roll(jnp.where(lane < 32, t2, t1), 64, 1),
        pltpu.roll(t2, 96, 1),
    ]
    return [jnp.where(lane < B, piece, 0.0) for piece in pieces]


def rows_of_b(tile, tail, tail_at):
    lane = lane_of(tile.shape[0])
    fifth = jnp.where(lane < 32, pltpu.roll(tile, 32, 1), pltpu.roll(tail, (32 - tail_at) % 128, 1))
    return [jnp.where(lane < B, piece, 0.0) for piece in (tile, fifth)]


def source_plane(base, e, d):
    return (base + 8 - d + e * (2 * d + 1)) & 7


def row_of(base, z, yx, r):
    delta = (z - base + 8) & 7
    e = jnp.where((delta >= 1) & (delta <= 4), 1, 0)
    d = jnp.where(e == 1, delta - 1, (8 - delta) & 7)
    return jnp.where(r < 4, e * 128 + yx * 16 + d * 4 + r, 256 + e * 64 + yx * 8 + d * 2 + r - 4)


def row_at(base, row):
    in_a, late = row < 256, row - 256
    e = jnp.where(in_a, row // 128, late // 64)
    yx = jnp.where(in_a, row % 128 // 16, late % 64 // 8)
    d = jnp.where(in_a, row % 16 // 4, late % 8 // 2)
    r = jnp.where(in_a, row % 4, 4 + late % 2)
    return source_plane(base, e, d), yx, r


def picks_outgoing(core, base):
    row = lax.broadcasted_iota(jnp.int32, (XLO * 128, YX * ROWS), 0)
    col = lax.broadcasted_iota(jnp.int32, (XLO * 128, YX * ROWS), 1)
    x_lo, jr = row // 128, row % 128
    z, yx, r = 4 * x_lo + 2 * core + jr // 48, jr % 48 // A, jr % A
    return jnp.where((col == row_of(base, z, yx, r)) & (jr < B), 1.0, 0.0).astype(BF16)


def picks_incoming(core, base):
    row = lax.broadcasted_iota(jnp.int32, (YX * ROWS, 4 * 128), 0)
    col = lax.broadcasted_iota(jnp.int32, (YX * ROWS, 4 * 128), 1)
    z, yx, r = row_at(base, row)
    other = jnp.bitwise_xor((z // 2) % 2, core)
    source = (other * 2 + z // 4) * 128 + (z % 2) * 48 + yx * A + r
    return jnp.where(col == source, 1.0, 0.0).astype(BF16)


def reorder(base, base_of_other):
    row = lax.broadcasted_iota(jnp.int32, (YX * ROWS, YX * ROWS), 0)
    col = lax.broadcasted_iota(jnp.int32, (YX * ROWS, YX * ROWS), 1)
    return jnp.where(col == row_of(base_of_other, *row_at(base, row)), 1.0, 0.0).astype(BF16)


def kernel(
    pair_hbm, proj_hbm, gate_hbm, out_hbm, o_ref,
    z_ref, proj_ref, gate_ref, out_ref, wide,
    senda, recva, send2, recv2, send1, recv1, spread, sendpa, sendpb, recvpa, recvpb, sendq, recvq, gather, sendx, recvx,
    load, zs, zr, ps, pr, cs, cr, qs, qr, xs, xr,
):
    loads = [
        pltpu.make_async_copy(src, dst, load.at[i])
        for i, (src, dst) in enumerate(
            ((pair_hbm, z_ref), (proj_hbm, proj_ref), (gate_hbm, gate_ref), (out_hbm, out_ref))
        )
    ]
    loads[0].start()
    loads[1].start()
    row, col = lax.axis_index("row"), lax.axis_index("col")
    plane, yx, x_lo, core = row >> 3, row & 7, col >> 1, col & 1
    chip = yx * XLO + x_lo
    chunk_of_chip = x_lo ^ ((yx >> 1) & 1)
    member = (plane + 8 - core) & 1
    base, base_of_other = (plane + 8 - member) & 7, (plane + 7 + member) & 7
    up = 1 - 2 * member
    relays = [((plane + 8 + step * up) & 7, d) for d, step in ((3, -3), (2, 2), (1, -1))]
    planes = [(plane + s) & (Z - 1) for s in FAR_PLANES]
    chips = [chip ^ s for s in FAR_CHIPS]

    def on_plane(other_plane):
        return {"row": other_plane * YX + yx, "col": col}

    def on_chip(other_chip, of_plane=plane):
        return {"row": of_plane * YX + (other_chip >> 1), "col": (other_chip & 1) * CORES + core}

    other_core = {"row": row, "col": col ^ 1}

    barrier = pltpu.get_barrier_semaphore()
    beside = (plane + 8 + up) & 7
    peers = [(hops, on_plane(peer)) for hops, peer in zip(PLANE_HOPS, planes)]
    peers += [(hops, on_chip(peer)) for hops, peer in zip(CHIP_HOPS, chips)]
    peers += [(hops + 1, on_chip(peer, beside)) for hops, peer in zip(CHIP_HOPS, chips)]
    peers = [peer for _, peer in sorted(peers, key=lambda peer: -peer[0])] + [other_core]
    for peer in peers:
        pl.semaphore_signal(barrier, inc=1, device_id=peer, device_id_type=MESH)
    loads[2].start()
    loads[3].start()

    sent = []

    def remote(src, dst, send, recv, peer):
        pltpu.make_async_remote_copy(
            src_ref=src, dst_ref=dst, send_sem=send, recv_sem=recv, device_id=peer, device_id_type=MESH
        ).start()

    def arrived(ref, sem):
        pltpu.make_async_copy(ref, ref, sem).wait()

    def slot_of(some_chip):
        return (some_chip & 1) * YX + (some_chip >> 1)

    def over_planes(src, dst, send, recv):
        for peer in planes:
            remote(src.at[peer], dst.at[plane], send, recv, on_plane(peer))
        pltpu.make_async_copy(src.at[plane], dst.at[plane], recv).start()
        sent.append((src.at[pl.ds(0, Z - 1)], send))

    def to_owners(chunk, src, dst, send, recv):
        here = dst.at[member * CHIPS + slot_of(chip)]

        def owner(m):
            return m * XLO + (chunk ^ ((m >> 1) & 1))

        for s in FAR_YX:
            peer = yx ^ s
            remote(src.at[1 - member, peer], here, send, recv, on_chip(owner(peer), beside))
            if s != 0:
                remote(src.at[member, peer], here, send, recv, on_chip(owner(peer)))
        own = chunk_of_chip == chunk

        @pl.when(own)
        def _():
            pltpu.make_async_copy(src.at[member, yx], here, recv).start()

        @pl.when(jnp.logical_not(own))
        def _():
            remote(src.at[member, yx], here, send, recv, on_chip(chip ^ 1))

    def wide_weights(u):
        for i in range(4):
            turned = proj_ref[u, i].astype(F32).T.reshape(Z, 2, HALF, C)
            for k in range(2):
                wide[u, k, i] = turned[:, k].reshape(Z * HALF, C).astype(BF16)

    def drain(count):
        for _ in range(count):
            arrived(*sent.pop(0))

    def z_parts(u):
        return [
            (senda.at[u, 0], recva.at[u, 0]),
            (send2.at[u], recv2.at[u]),
            (senda.at[u, 1], recva.at[u, 1]),
            (send1.at[u], recv1.at[u]),
        ]

    def issue(u, i):
        src, dst = z_parts(u)[i]
        for relay, d in relays:
            first = (relay + 8 - (member ^ (d & 1))) & 7
            for e in range(2):
                remote(src.at[(first + e) & 7], dst.at[2 * d + e], zs.at[u, i], zr.at[u, i], on_plane(relay))
        for e in range(2):
            pltpu.make_async_copy(src.at[(base + e) & 7], dst.at[e], zr.at[u, i]).start()
        sent.append((src.at[pl.ds(0, 6)], zs.at[u, i]))

    def edges(u, k, zn):
        both = dot(wide[u, k].reshape(4 * Z * HALF, C), zn, NT).reshape(4, Z, HALF, zn.shape[0])
        left = jax.nn.sigmoid(both[0]) * both[1]
        right = jax.nn.sigmoid(both[2]) * both[3]
        return jnp.concatenate([left, right], axis=1).astype(BF16)

    def head_a(u, rows):
        zn = normed(rows.reshape(4 * B, C), -1).astype(BF16)
        senda[u, 0] = edges(u, 0, zn)
        if u == 1:
            issue(u, 0)
        return zn

    def head_b(u, zn_a, rows):
        zn = normed(rows.reshape(2 * B, C), -1).astype(BF16)
        second = edges(u, 1, zn)
        send2[u, :, :, 0:192] = edges(u, 0, zn)
        send2[u, :, :, 192:256] = second[:, :, 128:192]
        send1[u] = second[:, :, 0:128]
        if u == 1:
            issue(u, 1)
        senda[u, 1] = edges(u, 1, zn_a)
        if u == 0:
            pl.semaphore_wait(barrier, len(peers))
            issue(u, 0)
            issue(u, 1)
        issue(u, 2)
        issue(u, 3)
        return zn

    def body(u, zn, before):
        if u == 0:
            wide_weights(1)
            loads[2].wait()
            loads[3].wait()
        gate = [jax.nn.sigmoid(dot(some, gate_ref[u])) for some in zn]
        picks = picks_outgoing(core, base) if u == 0 else picks_incoming(core, base)
        other_picks = picks_outgoing(core, base_of_other) if u == 0 else None
        in_order = reorder(base, base_of_other)
        drain(before)

        for k in range(2):
            for part in range(2):
                arrived(z_parts(u)[2 * k + part][1], zr.at[u, 2 * k + part])

                def spread_plane(p, carry):
                    if part == 0:
                        tiles = [recva[u, k, p, :, t * 128 : t * 128 + 128].astype(F32) for t in range(3)]
                        pieces = rows_of_a(tiles)
                    else:
                        tile = recv2[u, p, :, 0:128] if k == 0 else recv1[u, p]
                        pieces = rows_of_b(tile.astype(F32), recv2[u, p, :, 128:256].astype(F32), 64 * k)
                    d, e = p >> 1, p & 1
                    for i, piece in enumerate(pieces):
                        at = e * 2 * HALF * 24 + (d * 4 + i if part == 0 else 16 + d * 2 + i)
                        spread[u, k, pl.ds(at, 2 * HALF, stride=24), :] = piece
                    return carry

                lax.fori_loop(0, Z, spread_plane, 0, unroll=True)
                for e in range(2):
                    for m in range(HALF):
                        at = [(e * 2 * HALF + side * HALF + m) * 24 for side in range(2)]
                        if part == 0:
                            for side in range(2):
                                sendpa[u, k, e, m, side] = spread[u, k, at[side] : at[side] + 16, :].astype(BF16)
                        else:
                            both = [spread[u, k, at[side] + 16 : at[side] + 24, :] for side in range(2)]
                            sendpb[u, k, e, m] = jnp.concatenate(both, axis=0).astype(BF16)
                sendp, recvp = ((sendpa, recvpa), (sendpb, recvpb))[part]
                to_owners(k, sendp.at[u, k], recvp.at[u, 0], ps.at[u, part], pr.at[u, part])

        def shared(part, c):
            if u == 1 and part == 0:
                return recvpa.at[u, c, :, 0]
            return (recvpa, recvpb)[part].at[u, c]

        for part, recvp in enumerate((recvpa, recvpb)):
            sent.append((recvp.at[u, 0, pl.ds(0, 2 * CHIPS - 1)], ps.at[u, part]))
            arrived(recvp.at[u, 0], pr.at[u, part])
            remote(shared(part, 0), shared(part, 1), cs.at[u, part], cr.at[u, part], other_core)
            sent.append((shared(part, 0), cs.at[u, part]))

        def block_of(part, side, c, x):
            rows = []
            for e in range(2):
                slots = pl.ds(e * CHIPS + x * YX, YX)
                if part == 0:
                    rows.append(recvpa[u, c, slots, side].reshape(128, 128))
                else:
                    both = recvpb[u, c, slots].astype(F32)
                    rows.append(both[:, side * 8 : side * 8 + 8].reshape(64, 128).astype(BF16))
            return jnp.concatenate(rows, axis=0)

        def blocks(part, side, c):
            return jnp.concatenate([block_of(part, side, c, x) for x in range(XLO)], axis=1)

        halves, lefts = [], []
        for part in range(2):
            arrived(shared(part, 1), cr.at[u, part])
            here = slice(256 * part, 256 + 128 * part)
            left_of_other = dot(in_order[here, here], blocks(part, 0, 1)).astype(BF16)
            left = jnp.concatenate([blocks(part, 0, 0), left_of_other], axis=1)
            if u == 0:
                right = [dot(which[:, here], blocks(part, 1, c)) for c, which in enumerate((picks, other_picks))]
                halves.append(jnp.concatenate(right, axis=1))
                lefts.append(left)
            else:
                halves.append(dot(dot(picks, left, NT).astype(BF16), blocks(part, 1, 0)))
        tri = halves[0] + halves[1]
        if u == 0:
            tri = dot(jnp.concatenate(lefts, axis=0), tri.astype(BF16), NT)
        for x in range(XLO):
            block = tri[:, x * 128 : x * 128 + 128]
            slots = pl.ds(x * YX, YX)
            for e in range(2):
                part_a = block[e * 128 : e * 128 + 128].astype(BF16)
                sendq[u, slots, e * 16 : e * 16 + 16] = part_a.reshape(YX, 16, 128)
            part_b = block[256:384].reshape(2, YX, 8, 128)
            sendq[u, slots, 32:48] = jnp.concatenate([part_b[0], part_b[1]], axis=1).astype(BF16)
        here = recvq.at[u, chunk_of_chip, yx]
        for peer in chips:
            remote(sendq.at[u, slot_of(peer)], here, qs.at[u], qr.at[u, chunk_of_chip], on_chip(peer))
        pltpu.make_async_copy(sendq.at[u, slot_of(chip)], here, qr.at[u, chunk_of_chip]).start()
        sent.append((sendq.at[u, pl.ds(0, CHIPS - 1)], qs.at[u]))

        if u == 1:
            drain(len(sent))
        for k in range(2):
            arrived(recvq.at[u, k], qr.at[u, k])
            gather[u, k] = recvq[u, k].reshape(HALF * ROWS, 128).astype(F32)

            def gather_plane(p, carry):
                d, e = p >> 1, p & 1
                for r in range(0, A, 2):
                    at = e * 16 + d * 4 + r if r < 4 else 32 + e * 8 + d * 2
                    pair_of_rows = [gather[u, k, pl.ds(at + i, HALF, stride=ROWS), :] for i in range(2)]
                    tile = jnp.concatenate(pair_of_rows, axis=0).astype(BF16)
                    sendx[u, k, source_plane(base, e, d), r * HALF : r * HALF + 2 * HALF] = tile
                return carry

            lax.fori_loop(0, Z, gather_plane, 0, unroll=True)
            over_planes(sendx.at[u, k], recvx.at[u, k], xs.at[u, k], xr.at[u, k])
        for k in range(2):
            arrived(recvx.at[u, k], xr.at[u, k])
        return gate

    def ending(u, pair, gate, first):
        tri = [recvx[u, k, p].astype(F32) for p in range(Z) for k in range(2)]
        for r in range(pair.shape[0]):
            at = (first + r) * HALF
            tri_row = jnp.concatenate([part[at : at + HALF] for part in tri], axis=0)
            projected = dot(normed(tri_row, 0).astype(BF16), out_ref[u], TN)[:B]
            o_ref[first + r] = pair[r] + gate[r * B : r * B + B] * projected

    loads[1].wait()
    wide_weights(0)
    loads[0].wait()
    zn_a = head_a(0, z_ref[0:4])
    zn_b = head_b(0, zn_a, z_ref[4:6])
    gate_a, gate_b = body(0, (zn_a, zn_b), 0)
    ending(0, z_ref[0:4], gate_a, 0)
    before = len(sent)
    zn_a = head_a(1, o_ref[0:4])
    ending(0, z_ref[4:6], gate_b, 4)
    zn_b = head_b(1, zn_a, o_ref[4:6])
    gate_a, gate_b = body(1, (zn_a, zn_b), before)
    ending(1, o_ref[0:4], gate_a, 0)
    ending(1, o_ref[4:6], gate_b, 4)
    drain(len(sent))


def solution(mesh):
    vmem = pl.BlockSpec(memory_space=pltpu.VMEM)

    def per_device(*operands):
        pair_rep, proj_weights, gate_weights, out_weights = operands
        return pl.pallas_call(
            kernel,
            out_shape=jax.ShapeDtypeStruct(pair_rep.shape, pair_rep.dtype),
            in_specs=[pl.BlockSpec(memory_space=pltpu.HBM)] * 4,
            out_specs=vmem,
            scratch_shapes=[
                pltpu.VMEM(pair_rep.shape, F32),
                pltpu.VMEM(proj_weights.shape, BF16),
                pltpu.VMEM(gate_weights.shape, BF16),
                pltpu.VMEM(out_weights.shape, BF16),
                pltpu.VMEM((2, 2, 4, Z * HALF, C), BF16),
                pltpu.VMEM((2, 2, Z, 2 * HALF, 384), BF16),
                pltpu.VMEM((2, 2, Z, 2 * HALF, 384), BF16),
                pltpu.VMEM((2, Z, 2 * HALF, 256), BF16),
                pltpu.VMEM((2, Z, 2 * HALF, 256), BF16),
                pltpu.VMEM((2, Z, 2 * HALF, 128), BF16),
                pltpu.VMEM((2, Z, 2 * HALF, 128), BF16),
                pltpu.VMEM((2, 2, 2 * HALF * ROWS, 128), F32),
                pltpu.VMEM((2, 2, 2, HALF, 2, 16, 128), BF16),
                pltpu.VMEM((2, 2, 2, HALF, 16, 128), BF16),
                pltpu.VMEM((2, CORES, 2 * CHIPS, 2, 16, 128), BF16),
                pltpu.VMEM((2, CORES, 2 * CHIPS, 16, 128), BF16),
                pltpu.VMEM((2, CHIPS, ROWS, 128), BF16),
                pltpu.VMEM((2, 2, HALF, ROWS, 128), BF16),
                pltpu.VMEM((2, 2, HALF * ROWS, 128), F32),
                pltpu.VMEM((2, 2, Z, A * HALF, 128), BF16),
                pltpu.VMEM((2, 2, Z, A * HALF, 128), BF16),
                pltpu.SemaphoreType.DMA((4,)),
                pltpu.SemaphoreType.DMA((2, 4)),
                pltpu.SemaphoreType.DMA((2, 4)),
                pltpu.SemaphoreType.DMA((2, 2)),
                pltpu.SemaphoreType.DMA((2, 2)),
                pltpu.SemaphoreType.DMA((2, 2)),
                pltpu.SemaphoreType.DMA((2, 2)),
                pltpu.SemaphoreType.DMA((2,)),
                pltpu.SemaphoreType.DMA((2, 2)),
                pltpu.SemaphoreType.DMA((2, 2)),
                pltpu.SemaphoreType.DMA((2, 2)),
            ],
            compiler_params=pltpu.CompilerParams(
                collective_id=0, has_side_effects=True, vmem_limit_bytes=48 * 1024 * 1024
            ),
        )(*(pltpu.with_memory_space_constraint(x, pltpu.HBM) for x in operands))

    return jax.shard_map(
        per_device,
        mesh=mesh,
        in_specs=(P("row", "col", None), P(), P(), P()),
        out_specs=P("row", "col", None),
        check_vma=False,
    )
```

```python
import jax
import jax.numpy as jnp
from jax import lax
from jax.experimental import pallas as pl
from jax.experimental.pallas import tpu as pltpu
from jax.sharding import PartitionSpec as P

MESH = pl.DeviceIdType.MESH
F32, BF16 = jnp.float32, jnp.bfloat16
Z, CHIPS, YX, XLO, CORES = 8, 16, 8, 2, 2
A, B, C = 6, 96, 128
HALF = 8
POS = A * B
ROWS = Z * A
FAR_PLANES = (4, 3, 5, 2, 6, 1, 7)
FAR_CHIPS = (10, 11, 9, 14, 6, 8, 2, 15, 13, 7, 5, 12, 4, 3, 1)
PLANE_HOPS = (4, 3, 3, 2, 2, 1, 1)
CHIP_HOPS = (4, 3, 3, 3, 3, 2, 2, 2, 2, 2, 2, 1, 1, 1, 1)
FAR_YX = (5, 7, 3, 4, 1, 6, 2, 0)
NT = (((1,), (1,)), ((), ()))
TN = (((0,), (0,)), ((), ()))


def normed(values, axis):
    centred = values - jnp.mean(values, axis=axis, keepdims=True)
    variance = jnp.mean(centred * centred, axis=axis, keepdims=True)
    return centred * lax.rsqrt(variance + 1e-05)


def dot(a, b, dims=(((1,), (0,)), ((), ()))):
    return lax.dot_general(a, b, dims, preferred_element_type=F32)


def lane_of(rows):
    return lax.broadcasted_iota(jnp.int32, (rows, 128), 1)


def rows_of_a(tiles):
    lane = lane_of(tiles[0].shape[0])
    t0, t1, t2 = tiles
    pieces = [
        t0,
        pltpu.roll(jnp.where(lane < 64, t1, t0), 32, 1),
        pltpu.roll(jnp.where(lane < 32, t2, t1), 64, 1),
        pltpu.roll(t2, 96, 1),
    ]
    return [jnp.where(lane < B, piece, 0.0) for piece in pieces]


def rows_of_b(tile, tail, tail_at):
    lane = lane_of(tile.shape[0])
    fifth = jnp.where(lane < 32, pltpu.roll(tile, 32, 1), pltpu.roll(tail, (32 - tail_at) % 128, 1))
    return [jnp.where(lane < B, piece, 0.0) for piece in (tile, fifth)]


def source_plane(base, e, d):
    return (base + 8 - d + e * (2 * d + 1)) & 7


def row_of(base, z, yx, r):
    delta = (z - base + 8) & 7
    e = jnp.where((delta >= 1) & (delta <= 4), 1, 0)
    d = jnp.where(e == 1, delta - 1, (8 - delta) & 7)
    return jnp.where(r < 4, e * 128 + yx * 16 + d * 4 + r, 256 + e * 64 + yx * 8 + d * 2 + r - 4)


def row_at(base, row):
    in_a, late = row < 256, row - 256
    e = jnp.where(in_a, row // 128, late // 64)
    yx = jnp.where(in_a, row % 128 // 16, late % 64 // 8)
    d = jnp.where(in_a, row % 16 // 4, late % 8 // 2)
    r = jnp.where(in_a, row % 4, 4 + late % 2)
    return source_plane(base, e, d), yx, r


def picks_outgoing(core, base):
    row = lax.broadcasted_iota(jnp.int32, (XLO * 128, YX * ROWS), 0)
    col = lax.broadcasted_iota(jnp.int32, (XLO * 128, YX * ROWS), 1)
    x_lo, jr = row // 128, row % 128
    z, yx, r = 4 * x_lo + 2 * core + jr // 48, jr % 48 // A, jr % A
    return jnp.where((col == row_of(base, z, yx, r)) & (jr < B), 1.0, 0.0).astype(BF16)


def picks_incoming(core, base):
    row = lax.broadcasted_iota(jnp.int32, (YX * ROWS, 4 * 128), 0)
    col = lax.broadcasted_iota(jnp.int32, (YX * ROWS, 4 * 128), 1)
    z, yx, r = row_at(base, row)
    other = jnp.bitwise_xor((z // 2) % 2, core)
    source = (other * 2 + z // 4) * 128 + (z % 2) * 48 + yx * A + r
    return jnp.where(col == source, 1.0, 0.0).astype(BF16)


def reorder(base, base_of_other):
    row = lax.broadcasted_iota(jnp.int32, (YX * ROWS, YX * ROWS), 0)
    col = lax.broadcasted_iota(jnp.int32, (YX * ROWS, YX * ROWS), 1)
    return jnp.where(col == row_of(base_of_other, *row_at(base, row)), 1.0, 0.0).astype(BF16)


def kernel(
    pair_hbm, proj_hbm, gate_hbm, out_hbm, o_ref,
    z_ref, proj_ref, gate_ref, out_ref, wide,
    senda, recva, send2, recv2, send1, recv1, spread, sendpa, sendpb, recvpa, recvpb, sendq, recvq, gather, sendx, recvx,
    load, zs, zr, ps, pr, cs, cr, qs, qr, xs, xr,
):
    loads = [
        pltpu.make_async_copy(src, dst, load.at[i])
        for i, (src, dst) in enumerate(
            ((pair_hbm, z_ref), (proj_hbm, proj_ref), (gate_hbm, gate_ref), (out_hbm, out_ref))
        )
    ]
    loads[0].start()
    loads[1].start()
    row, col = lax.axis_index("row"), lax.axis_index("col")
    plane, yx, x_lo, core = row >> 3, row & 7, col >> 1, col & 1
    chip = yx * XLO + x_lo
    chunk_of_chip = x_lo ^ ((yx >> 1) & 1)
    member = (plane + 8 - core) & 1
    base, base_of_other = (plane + 8 - member) & 7, (plane + 7 + member) & 7
    up = 1 - 2 * member
    relays = [((plane + 8 + step * up) & 7, d) for d, step in ((3, -3), (2, 2), (1, -1))]
    planes = [(plane + s) & (Z - 1) for s in FAR_PLANES]
    chips = [chip ^ s for s in FAR_CHIPS]

    def on_plane(other_plane):
        return {"row": other_plane * YX + yx, "col": col}

    def on_chip(other_chip, of_plane=plane):
        return {"row": of_plane * YX + (other_chip >> 1), "col": (other_chip & 1) * CORES + core}

    other_core = {"row": row, "col": col ^ 1}

    barrier = pltpu.get_barrier_semaphore()
    beside = (plane + 8 + up) & 7
    peers = [(hops, on_plane(peer)) for hops, peer in zip(PLANE_HOPS, planes)]
    peers += [(hops, on_chip(peer)) for hops, peer in zip(CHIP_HOPS, chips)]
    peers += [(hops + 1, on_chip(peer, beside)) for hops, peer in zip(CHIP_HOPS, chips)]
    peers = [peer for _, peer in sorted(peers, key=lambda peer: -peer[0])] + [other_core]
    for peer in peers:
        pl.semaphore_signal(barrier, inc=1, device_id=peer, device_id_type=MESH)
    loads[2].start()
    loads[3].start()

    sent = []

    def remote(src, dst, send, recv, peer):
        pltpu.make_async_remote_copy(
            src_ref=src, dst_ref=dst, send_sem=send, recv_sem=recv, device_id=peer, device_id_type=MESH
        ).start()

    def arrived(ref, sem):
        pltpu.make_async_copy(ref, ref, sem).wait()

    def slot_of(some_chip):
        return (some_chip & 1) * YX + (some_chip >> 1)

    def over_planes(src, dst, send, recv):
        for peer in planes:
            remote(src.at[peer], dst.at[plane], send, recv, on_plane(peer))
        pltpu.make_async_copy(src.at[plane], dst.at[plane], recv).start()
        sent.append((src.at[pl.ds(0, Z - 1)], send))

    def to_owners(chunk, src, dst, send, recv):
        here = dst.at[member * CHIPS + slot_of(chip)]

        def owner(m):
            return m * XLO + (chunk ^ ((m >> 1) & 1))

        for s in FAR_YX:
            peer = yx ^ s
            remote(src.at[1 - member, peer], here, send, recv, on_chip(owner(peer), beside))
            if s != 0:
                remote(src.at[member, peer], here, send, recv, on_chip(owner(peer)))
        own = chunk_of_chip == chunk

        @pl.when(own)
        def _():
            pltpu.make_async_copy(src.at[member, yx], here, recv).start()

        @pl.when(jnp.logical_not(own))
        def _():
            remote(src.at[member, yx], here, send, recv, on_chip(chip ^ 1))

    def wide_weights(u):
        for i in range(4):
            turned = proj_ref[u, i].astype(F32).T.reshape(Z, 2, HALF, C)
            for k in range(2):
                wide[u, k, i] = turned[:, k].reshape(Z * HALF, C).astype(BF16)

    def drain(count):
        for _ in range(count):
            arrived(*sent.pop(0))

    def z_parts(u):
        return [
            (senda.at[u, 0], recva.at[u, 0]),
            (send2.at[u], recv2.at[u]),
            (senda.at[u, 1], recva.at[u, 1]),
            (send1.at[u], recv1.at[u]),
        ]

    def issue(u, i):
        src, dst = z_parts(u)[i]
        for relay, d in relays:
            first = (relay + 8 - (member ^ (d & 1))) & 7
            for e in range(2):
                remote(src.at[(first + e) & 7], dst.at[2 * d + e], zs.at[u, i], zr.at[u, i], on_plane(relay))
        for e in range(2):
            pltpu.make_async_copy(src.at[(base + e) & 7], dst.at[e], zr.at[u, i]).start()
        sent.append((src.at[pl.ds(0, 6)], zs.at[u, i]))

    def edges(u, k, zn):
        both = dot(wide[u, k].reshape(4 * Z * HALF, C), zn, NT).reshape(4, Z, HALF, zn.shape[0])
        left = jax.nn.sigmoid(both[0]) * both[1]
        right = jax.nn.sigmoid(both[2]) * both[3]
        return jnp.concatenate([left, right], axis=1).astype(BF16)

    def head_a(u, rows):
        zn = normed(rows.reshape(4 * B, C), -1).astype(BF16)
        senda[u, 0] = edges(u, 0, zn)
        if u == 1:
            issue(u, 0)
        return zn

    def head_b(u, zn_a, rows):
        zn = normed(rows.reshape(2 * B, C), -1).astype(BF16)
        second = edges(u, 1, zn)
        send2[u, :, :, 0:192] = edges(u, 0, zn)
        send2[u, :, :, 192:256] = second[:, :, 128:192]
        send1[u] = second[:, :, 0:128]
        if u == 1:
            issue(u, 1)
        senda[u, 1] = edges(u, 1, zn_a)
        if u == 0:
            pl.semaphore_wait(barrier, len(peers))
            issue(u, 0)
            issue(u, 1)
        issue(u, 2)
        issue(u, 3)
        return zn

    def body(u, zn, before):
        if u == 0:
            wide_weights(1)
            loads[2].wait()
            loads[3].wait()
        gate = [jax.nn.sigmoid(dot(some, gate_ref[u])) for some in zn]
        picks = picks_outgoing(core, base) if u == 0 else picks_incoming(core, base)
        other_picks = picks_outgoing(core, base_of_other) if u == 0 else None
        in_order = reorder(base, base_of_other)
        drain(before)

        for k in range(2):
            for part in range(2):
                arrived(z_parts(u)[2 * k + part][1], zr.at[u, 2 * k + part])

                def spread_plane(p, carry):
                    if part == 0:
                        tiles = [recva[u, k, p, :, t * 128 : t * 128 + 128].astype(F32) for t in range(3)]
                        pieces = rows_of_a(tiles)
                    else:
                        tile = recv2[u, p, :, 0:128] if k == 0 else recv1[u, p]
                        pieces = rows_of_b(tile.astype(F32), recv2[u, p, :, 128:256].astype(F32), 64 * k)
                    d, e = p >> 1, p & 1
                    for i, piece in enumerate(pieces):
                        at = e * 2 * HALF * 24 + (d * 4 + i if part == 0 else 16 + d * 2 + i)
                        spread[u, k, pl.ds(at, 2 * HALF, stride=24), :] = piece
                    return carry

                lax.fori_loop(0, Z, spread_plane, 0, unroll=True)
                for e in range(2):
                    for m in range(HALF):
                        at = [(e * 2 * HALF + side * HALF + m) * 24 for side in range(2)]
                        if part == 0:
                            for side in range(2):
                                sendpa[u, k, e, m, side] = spread[u, k, at[side] : at[side] + 16, :].astype(BF16)
                        else:
                            both = [spread[u, k, at[side] + 16 : at[side] + 24, :] for side in range(2)]
                            sendpb[u, k, e, m] = jnp.concatenate(both, axis=0).astype(BF16)
                sendp, recvp = ((sendpa, recvpa), (sendpb, recvpb))[part]
                to_owners(k, sendp.at[u, k], recvp.at[u, 0], ps.at[u, part], pr.at[u, part])

        def shared(part, c):
            if u == 1 and part == 0:
                return recvpa.at[u, c, :, 0]
            return (recvpa, recvpb)[part].at[u, c]

        for part, recvp in enumerate((recvpa, recvpb)):
            sent.append((recvp.at[u, 0, pl.ds(0, 2 * CHIPS - 1)], ps.at[u, part]))
            arrived(recvp.at[u, 0], pr.at[u, part])
            remote(shared(part, 0), shared(part, 1), cs.at[u, part], cr.at[u, part], other_core)
            sent.append((shared(part, 0), cs.at[u, part]))

        def block_of(part, side, c, x):
            rows = []
            for e in range(2):
                slots = pl.ds(e * CHIPS + x * YX, YX)
                if part == 0:
                    rows.append(recvpa[u, c, slots, side].reshape(128, 128))
                else:
                    both = recvpb[u, c, slots].astype(F32)
                    rows.append(both[:, side * 8 : side * 8 + 8].reshape(64, 128).astype(BF16))
            return jnp.concatenate(rows, axis=0)

        def blocks(part, side, c):
            return jnp.concatenate([block_of(part, side, c, x) for x in range(XLO)], axis=1)

        halves, lefts = [], []
        for part in range(2):
            arrived(shared(part, 1), cr.at[u, part])
            here = slice(256 * part, 256 + 128 * part)
            left_of_other = dot(in_order[here, here], blocks(part, 0, 1)).astype(BF16)
            left = jnp.concatenate([blocks(part, 0, 0), left_of_other], axis=1)
            if u == 0:
                right = [dot(which[:, here], blocks(part, 1, c)) for c, which in enumerate((picks, other_picks))]
                halves.append(jnp.concatenate(right, axis=1))
                lefts.append(left)
            else:
                halves.append(dot(dot(picks, left, NT).astype(BF16), blocks(part, 1, 0)))
        tri = halves[0] + halves[1]
        if u == 0:
            tri = dot(jnp.concatenate(lefts, axis=0), tri.astype(BF16), NT)
        for x in range(XLO):
            block = tri[:, x * 128 : x * 128 + 128]
            slots = pl.ds(x * YX, YX)
            for e in range(2):
                part_a = block[e * 128 : e * 128 + 128].astype(BF16)
                sendq[u, slots, e * 16 : e * 16 + 16] = part_a.reshape(YX, 16, 128)
            part_b = block[256:384].reshape(2, YX, 8, 128)
            sendq[u, slots, 32:48] = jnp.concatenate([part_b[0], part_b[1]], axis=1).astype(BF16)
        here = recvq.at[u, chunk_of_chip, yx]
        for peer in chips:
            remote(sendq.at[u, slot_of(peer)], here, qs.at[u], qr.at[u, chunk_of_chip], on_chip(peer))
        pltpu.make_async_copy(sendq.at[u, slot_of(chip)], here, qr.at[u, chunk_of_chip]).start()
        sent.append((sendq.at[u, pl.ds(0, CHIPS - 1)], qs.at[u]))

        if u == 1:
            drain(len(sent))
        for k in range(2):
            arrived(recvq.at[u, k], qr.at[u, k])
            gather[u, k, 0 : HALF * ROWS] = recvq[u, k].reshape(HALF * ROWS, 128).astype(F32)

            def gather_plane(p, carry):
                d, e = p >> 1, p & 1
                for r in range(0, A, 2):
                    at = e * 16 + d * 4 + r if r < 4 else 32 + e * 8 + d * 2
                    pair_of_rows = [gather[u, k, pl.ds(at + i, HALF, stride=ROWS), :] for i in range(2)]
                    tile = jnp.concatenate(pair_of_rows, axis=0).astype(BF16)
                    sendx[u, k, source_plane(base, e, d), r * HALF : r * HALF + 2 * HALF] = tile
                return carry

            lax.fori_loop(0, Z, gather_plane, 0, unroll=True)
            over_planes(sendx.at[u, k], recvx.at[u, k], xs.at[u, k], xr.at[u, k])
        for k in range(2):
            arrived(recvx.at[u, k], xr.at[u, k])
        return gate

    def ending(u, pair, gate, first):
        tri = [recvx[u, k, p].astype(F32) for p in range(Z) for k in range(2)]
        for r in range(pair.shape[0]):
            at = (first + r) * HALF
            tri_row = jnp.concatenate([part[at : at + HALF] for part in tri], axis=0)
            projected = dot(normed(tri_row, 0).astype(BF16), out_ref[u], TN)[:B]
            o_ref[first + r] = pair[r] + gate[r * B : r * B + B] * projected

    loads[1].wait()
    wide_weights(0)
    loads[0].wait()
    zn_a = head_a(0, z_ref[0:4])
    zn_b = head_b(0, zn_a, z_ref[4:6])
    gate_a, gate_b = body(0, (zn_a, zn_b), 0)
    ending(0, z_ref[0:4], gate_a, 0)
    before = len(sent)
    zn_a = head_a(1, o_ref[0:4])
    ending(0, z_ref[4:6], gate_b, 4)
    zn_b = head_b(1, zn_a, o_ref[4:6])
    gate_a, gate_b = body(1, (zn_a, zn_b), before)
    ending(1, o_ref[0:4], gate_a, 0)
    ending(1, o_ref[4:6], gate_b, 4)
    drain(len(sent))


def solution(mesh):
    vmem = pl.BlockSpec(memory_space=pltpu.VMEM)

    def per_device(*operands):
        pair_rep, proj_weights, gate_weights, out_weights = operands
        return pl.pallas_call(
            kernel,
            out_shape=jax.ShapeDtypeStruct(pair_rep.shape, pair_rep.dtype),
            in_specs=[pl.BlockSpec(memory_space=pltpu.HBM)] * 4,
            out_specs=vmem,
            scratch_shapes=[
                pltpu.VMEM(pair_rep.shape, F32),
                pltpu.VMEM(proj_weights.shape, BF16),
                pltpu.VMEM(gate_weights.shape, BF16),
                pltpu.VMEM(out_weights.shape, BF16),
                pltpu.VMEM((2, 2, 4, Z * HALF, C), BF16),
                pltpu.VMEM((2, 2, Z, 2 * HALF, 384), BF16),
                pltpu.VMEM((2, 2, Z, 2 * HALF, 384), BF16),
                pltpu.VMEM((2, Z, 2 * HALF, 256), BF16),
                pltpu.VMEM((2, Z, 2 * HALF, 256), BF16),
                pltpu.VMEM((2, Z, 2 * HALF, 128), BF16),
                pltpu.VMEM((2, Z, 2 * HALF, 128), BF16),
                pltpu.VMEM((2, 2, 2 * HALF * ROWS + 24, 128), F32),
                pltpu.VMEM((2, 2, 2, HALF, 2, 16, 128), BF16),
                pltpu.VMEM((2, 2, 2, HALF, 16, 128), BF16),
                pltpu.VMEM((2, CORES, 2 * CHIPS, 2, 16, 128), BF16),
                pltpu.VMEM((2, CORES, 2 * CHIPS, 16, 128), BF16),
                pltpu.VMEM((2, CHIPS, ROWS, 128), BF16),
                pltpu.VMEM((2, 2, HALF, ROWS, 128), BF16),
                pltpu.VMEM((2, 2, HALF * ROWS + ROWS, 128), F32),
                pltpu.VMEM((2, 2, Z, A * HALF, 128), BF16),
                pltpu.VMEM((2, 2, Z, A * HALF, 128), BF16),
                pltpu.SemaphoreType.DMA((4,)),
                pltpu.SemaphoreType.DMA((2, 4)),
                pltpu.SemaphoreType.DMA((2, 4)),
                pltpu.SemaphoreType.DMA((2, 2)),
                pltpu.SemaphoreType.DMA((2, 2)),
                pltpu.SemaphoreType.DMA((2, 2)),
                pltpu.SemaphoreType.DMA((2, 2)),
                pltpu.SemaphoreType.DMA((2,)),
                pltpu.SemaphoreType.DMA((2, 2)),
                pltpu.SemaphoreType.DMA((2, 2)),
                pltpu.SemaphoreType.DMA((2, 2)),
            ],
            compiler_params=pltpu.CompilerParams(
                collective_id=0, has_side_effects=True, vmem_limit_bytes=48 * 1024 * 1024
            ),
        )(*(pltpu.with_memory_space_constraint(x, pltpu.HBM) for x in operands))

    return jax.shard_map(
        per_device,
        mesh=mesh,
        in_specs=(P("row", "col", None), P(), P(), P()),
        out_specs=P("row", "col", None),
        check_vma=False,
    )
```

```python
import jax
import jax.numpy as jnp
from jax import lax
from jax.experimental import pallas as pl
from jax.experimental.pallas import tpu as pltpu
from jax.sharding import PartitionSpec as P

MESH = pl.DeviceIdType.MESH
F32, BF16 = jnp.float32, jnp.bfloat16
Z, CHIPS, YX, XLO, CORES = 8, 16, 8, 2, 2
A, B, C = 6, 96, 128
HALF = 8
POS = A * B
ROWS = Z * A
FAR_PLANES = (4, 3, 5, 2, 6, 1, 7)
FAR_CHIPS = (10, 11, 9, 14, 6, 8, 2, 15, 13, 7, 5, 12, 4, 3, 1)
PLANE_HOPS = (4, 3, 3, 2, 2, 1, 1)
CHIP_HOPS = (4, 3, 3, 3, 3, 2, 2, 2, 2, 2, 2, 1, 1, 1, 1)
FAR_YX = (5, 7, 3, 4, 1, 6, 2, 0)
NT = (((1,), (1,)), ((), ()))
TN = (((0,), (0,)), ((), ()))


def normed(values, axis):
    centred = values - jnp.mean(values, axis=axis, keepdims=True)
    variance = jnp.mean(centred * centred, axis=axis, keepdims=True)
    return centred * lax.rsqrt(variance + 1e-05)


def dot(a, b, dims=(((1,), (0,)), ((), ()))):
    return lax.dot_general(a, b, dims, preferred_element_type=F32)


def lane_of(rows):
    return lax.broadcasted_iota(jnp.int32, (rows, 128), 1)


def rows_of_a(tiles):
    lane = lane_of(tiles[0].shape[0])
    t0, t1, t2 = tiles
    pieces = [
        t0,
        pltpu.roll(jnp.where(lane < 64, t1, t0), 32, 1),
        pltpu.roll(jnp.where(lane < 32, t2, t1), 64, 1),
        pltpu.roll(t2, 96, 1),
    ]
    return [jnp.where(lane < B, piece, 0.0) for piece in pieces]


def rows_of_b(tile, tail, tail_at):
    lane = lane_of(tile.shape[0])
    fifth = jnp.where(lane < 32, pltpu.roll(tile, 32, 1), pltpu.roll(tail, (32 - tail_at) % 128, 1))
    return [jnp.where(lane < B, piece, 0.0) for piece in (tile, fifth)]


def source_plane(base, e, d):
    return (base + 8 - d + e * (2 * d + 1)) & 7


def row_of(base, z, yx, r):
    delta = (z - base + 8) & 7
    e = jnp.where((delta >= 1) & (delta <= 4), 1, 0)
    d = jnp.where(e == 1, delta - 1, (8 - delta) & 7)
    return jnp.where(r < 4, e * 128 + yx * 16 + d * 4 + r, 256 + e * 64 + yx * 8 + d * 2 + r - 4)


def row_at(base, row):
    in_a, late = row < 256, row - 256
    e = jnp.where(in_a, row // 128, late // 64)
    yx = jnp.where(in_a, row % 128 // 16, late % 64 // 8)
    d = jnp.where(in_a, row % 16 // 4, late % 8 // 2)
    r = jnp.where(in_a, row % 4, 4 + late % 2)
    return source_plane(base, e, d), yx, r


def picks_outgoing(core, base):
    row = lax.broadcasted_iota(jnp.int32, (XLO * 128, YX * ROWS), 0)
    col = lax.broadcasted_iota(jnp.int32, (XLO * 128, YX * ROWS), 1)
    x_lo, jr = row // 128, row % 128
    z, yx, r = 4 * x_lo + 2 * core + jr // 48, jr % 48 // A, jr % A
    return jnp.where((col == row_of(base, z, yx, r)) & (jr < B), 1.0, 0.0).astype(BF16)


def picks_incoming(core, base):
    row = lax.broadcasted_iota(jnp.int32, (YX * ROWS, 4 * 128), 0)
    col = lax.broadcasted_iota(jnp.int32, (YX * ROWS, 4 * 128), 1)
    z, yx, r = row_at(base, row)
    other = jnp.bitwise_xor((z // 2) % 2, core)
    source = (other * 2 + z // 4) * 128 + (z % 2) * 48 + yx * A + r
    return jnp.where(col == source, 1.0, 0.0).astype(BF16)


def reorder(base, base_of_other):
    row = lax.broadcasted_iota(jnp.int32, (YX * ROWS, YX * ROWS), 0)
    col = lax.broadcasted_iota(jnp.int32, (YX * ROWS, YX * ROWS), 1)
    return jnp.where(col == row_of(base_of_other, *row_at(base, row)), 1.0, 0.0).astype(BF16)


def kernel(
    pair_hbm, proj_hbm, gate_hbm, out_hbm, o_ref,
    z_ref, proj_ref, gate_ref, out_ref, wide,
    senda, recva, send2, recv2, send1, recv1, spread, sendpa, sendpb, recvpa, recvpb, sendq, recvq, gather, sendx, recvx,
    load, zs, zr, ps, pr, cs, cr, qs, qr, xs, xr,
):
    loads = [
        pltpu.make_async_copy(src, dst, load.at[i])
        for i, (src, dst) in enumerate(
            ((pair_hbm, z_ref), (proj_hbm, proj_ref), (gate_hbm, gate_ref), (out_hbm, out_ref))
        )
    ]
    loads[0].start()
    loads[1].start()
    row, col = lax.axis_index("row"), lax.axis_index("col")
    plane, yx, x_lo, core = row >> 3, row & 7, col >> 1, col & 1
    chip = yx * XLO + x_lo
    chunk_of_chip = x_lo ^ ((yx >> 1) & 1)
    member = (plane + 8 - core) & 1
    base, base_of_other = (plane + 8 - member) & 7, (plane + 7 + member) & 7
    up = 1 - 2 * member
    relays = [((plane + 8 + step * up) & 7, d) for d, step in ((3, -3), (2, 2), (1, -1))]
    planes = [(plane + s) & (Z - 1) for s in FAR_PLANES]
    chips = [chip ^ s for s in FAR_CHIPS]

    def on_plane(other_plane):
        return {"row": other_plane * YX + yx, "col": col}

    def on_chip(other_chip, of_plane=plane):
        return {"row": of_plane * YX + (other_chip >> 1), "col": (other_chip & 1) * CORES + core}

    other_core = {"row": row, "col": col ^ 1}

    barrier = pltpu.get_barrier_semaphore()
    beside = (plane + 8 + up) & 7
    peers = [(hops, on_plane(peer)) for hops, peer in zip(PLANE_HOPS, planes)]
    peers += [(hops, on_chip(peer)) for hops, peer in zip(CHIP_HOPS, chips)]
    peers += [(hops + 1, on_chip(peer, beside)) for hops, peer in zip(CHIP_HOPS, chips)]
    peers = [peer for _, peer in sorted(peers, key=lambda peer: -peer[0])] + [other_core]
    for peer in peers:
        pl.semaphore_signal(barrier, inc=1, device_id=peer, device_id_type=MESH)
    loads[2].start()
    loads[3].start()

    sent = []

    def remote(src, dst, send, recv, peer):
        pltpu.make_async_remote_copy(
            src_ref=src, dst_ref=dst, send_sem=send, recv_sem=recv, device_id=peer, device_id_type=MESH
        ).start()

    def arrived(ref, sem):
        pltpu.make_async_copy(ref, ref, sem).wait()

    def slot_of(some_chip):
        return (some_chip & 1) * YX + (some_chip >> 1)

    def over_planes(src, dst, send, recv):
        for peer in planes:
            remote(src.at[peer], dst.at[plane], send, recv, on_plane(peer))
        pltpu.make_async_copy(src.at[plane], dst.at[plane], recv).start()
        sent.append((src.at[pl.ds(0, Z - 1)], send))

    def to_owners(chunk, src, dst, send, recv):
        here = dst.at[member * CHIPS + slot_of(chip)]

        def owner(m):
            return m * XLO + (chunk ^ ((m >> 1) & 1))

        for s in FAR_YX:
            peer = yx ^ s
            remote(src.at[1 - member, peer], here, send, recv, on_chip(owner(peer), beside))
            if s != 0:
                remote(src.at[member, peer], here, send, recv, on_chip(owner(peer)))
        own = chunk_of_chip == chunk

        @pl.when(own)
        def _():
            pltpu.make_async_copy(src.at[member, yx], here, recv).start()

        @pl.when(jnp.logical_not(own))
        def _():
            remote(src.at[member, yx], here, send, recv, on_chip(chip ^ 1))

    def wide_weights(u):
        for i in range(4):
            turned = proj_ref[u, i].astype(F32).T.reshape(Z, 2, HALF, C)
            for k in range(2):
                wide[u, k, i] = turned[:, k].reshape(Z * HALF, C).astype(BF16)

    def drain(count):
        for _ in range(count):
            arrived(*sent.pop(0))

    def z_parts(u):
        return [
            (senda.at[u, 0], recva.at[u, 0]),
            (send2.at[u], recv2.at[u]),
            (senda.at[u, 1], recva.at[u, 1]),
            (send1.at[u], recv1.at[u]),
        ]

    def issue(u, i):
        src, dst = z_parts(u)[i]
        for relay, d in relays:
            first = (relay + 8 - (member ^ (d & 1))) & 7
            for e in range(2):
                remote(src.at[(first + e) & 7], dst.at[2 * d + e], zs.at[u, i], zr.at[u, i], on_plane(relay))
        for e in range(2):
            pltpu.make_async_copy(src.at[(base + e) & 7], dst.at[e], zr.at[u, i]).start()
        sent.append((src.at[pl.ds(0, 6)], zs.at[u, i]))

    def edges(u, k, zn):
        both = dot(wide[u, k].reshape(4 * Z * HALF, C), zn, NT).reshape(4, Z, HALF, zn.shape[0])
        left = jax.nn.sigmoid(both[0]) * both[1]
        right = jax.nn.sigmoid(both[2]) * both[3]
        return jnp.concatenate([left, right], axis=1).astype(BF16)

    def head_a(u, rows):
        zn = normed(rows.reshape(4 * B, C), -1).astype(BF16)
        senda[u, 0] = edges(u, 0, zn)
        if u == 1:
            issue(u, 0)
        return zn

    def head_b(u, zn_a, rows):
        zn = normed(rows.reshape(2 * B, C), -1).astype(BF16)
        second = edges(u, 1, zn)
        send2[u, :, :, 0:192] = edges(u, 0, zn)
        send2[u, :, :, 192:256] = second[:, :, 128:192]
        send1[u] = second[:, :, 0:128]
        if u == 1:
            issue(u, 1)
        senda[u, 1] = edges(u, 1, zn_a)
        if u == 0:
            pl.semaphore_wait(barrier, len(peers))
            issue(u, 0)
            issue(u, 1)
        issue(u, 2)
        issue(u, 3)
        return zn

    def body(u, zn, before):
        if u == 0:
            wide_weights(1)
            loads[2].wait()
            loads[3].wait()
        gate = [jax.nn.sigmoid(dot(some, gate_ref[u])) for some in zn]
        picks = picks_outgoing(core, base) if u == 0 else picks_incoming(core, base)
        other_picks = picks_outgoing(core, base_of_other) if u == 0 else None
        in_order = reorder(base, base_of_other)
        drain(before)

        for k in range(2):
            for part in range(2):
                arrived(z_parts(u)[2 * k + part][1], zr.at[u, 2 * k + part])

                def spread_plane(p, carry):
                    if part == 0:
                        tiles = [recva[u, k, p, :, t * 128 : t * 128 + 128].astype(F32) for t in range(3)]
                        pieces = rows_of_a(tiles)
                    else:
                        tile = recv2[u, p, :, 0:128] if k == 0 else recv1[u, p]
                        pieces = rows_of_b(tile.astype(F32), recv2[u, p, :, 128:256].astype(F32), 64 * k)
                    d, e = p >> 1, p & 1
                    for i, piece in enumerate(pieces):
                        at = e * 2 * HALF * 24 + (d * 4 + i if part == 0 else 16 + d * 2 + i)
                        spread[u, k, pl.ds(at, 2 * HALF, stride=24), :] = piece
                    return carry

                lax.fori_loop(0, Z, spread_plane, 0, unroll=True)
                for e in range(2):
                    for m in range(HALF):
                        at = [(e * 2 * HALF + side * HALF + m) * 24 for side in range(2)]
                        if part == 0:
                            for side in range(2):
                                sendpa[u, k, e, m, side] = spread[u, k, at[side] : at[side] + 16, :].astype(BF16)
                        else:
                            both = [spread[u, k, at[side] + 16 : at[side] + 24, :] for side in range(2)]
                            sendpb[u, k, e, m] = jnp.concatenate(both, axis=0).astype(BF16)
                sendp, recvp = ((sendpa, recvpa), (sendpb, recvpb))[part]
                to_owners(k, sendp.at[u, k], recvp.at[u, 0], ps.at[u, part], pr.at[u, part])

        def shared(part, c):
            if u == 1 and part == 0:
                return recvpa.at[u, c, :, 0]
            return (recvpa, recvpb)[part].at[u, c]

        for part, recvp in enumerate((recvpa, recvpb)):
            sent.append((recvp.at[u, 0, pl.ds(0, 2 * CHIPS - 1)], ps.at[u, part]))
            arrived(recvp.at[u, 0], pr.at[u, part])
            remote(shared(part, 0), shared(part, 1), cs.at[u, part], cr.at[u, part], other_core)
            sent.append((shared(part, 0), cs.at[u, part]))

        def block_of(part, side, c, x):
            rows = []
            for e in range(2):
                slots = pl.ds(e * CHIPS + x * YX, YX)
                if part == 0:
                    rows.append(recvpa[u, c, slots, side].reshape(128, 128))
                else:
                    both = recvpb[u, c, slots].astype(F32)
                    rows.append(both[:, side * 8 : side * 8 + 8].reshape(64, 128).astype(BF16))
            return jnp.concatenate(rows, axis=0)

        def blocks(part, side, c):
            return jnp.concatenate([block_of(part, side, c, x) for x in range(XLO)], axis=1)

        halves, lefts = [], []
        for part in range(2):
            arrived(shared(part, 1), cr.at[u, part])
            here = slice(256 * part, 256 + 128 * part)
            left_of_other = dot(in_order[here, here], blocks(part, 0, 1)).astype(BF16)
            left = jnp.concatenate([blocks(part, 0, 0), left_of_other], axis=1)
            if u == 0:
                right = [dot(which[:, here], blocks(part, 1, c)) for c, which in enumerate((picks, other_picks))]
                halves.append(jnp.concatenate(right, axis=1))
                lefts.append(left)
            else:
                halves.append(dot(dot(picks, left, NT).astype(BF16), blocks(part, 1, 0)))
        tri = halves[0] + halves[1]
        if u == 0:
            tri = dot(jnp.concatenate(lefts, axis=0), tri.astype(BF16), NT)
        for x in range(XLO):
            block = tri[:, x * 128 : x * 128 + 128]
            slots = pl.ds(x * YX, YX)
            for e in range(2):
                part_a = block[e * 128 : e * 128 + 128].astype(BF16)
                sendq[u, slots, e * 16 : e * 16 + 16] = part_a.reshape(YX, 16, 128)
            part_b = block[256:384].reshape(2, YX, 8, 128)
            sendq[u, slots, 32:48] = jnp.concatenate([part_b[0], part_b[1]], axis=1).astype(BF16)
        drain(len(sent))
        here = recvq.at[u, chunk_of_chip, yx]
        for peer in chips:
            remote(sendq.at[u, slot_of(peer)], here, qs.at[u], qr.at[u, chunk_of_chip], on_chip(peer))
        pltpu.make_async_copy(sendq.at[u, slot_of(chip)], here, qr.at[u, chunk_of_chip]).start()
        sent.append((sendq.at[u, pl.ds(0, CHIPS - 1)], qs.at[u]))

        if u == 1:
            drain(len(sent))
        for k in range(2):
            arrived(recvq.at[u, k], qr.at[u, k])
            gather[u, k, 0 : HALF * ROWS] = recvq[u, k].reshape(HALF * ROWS, 128).astype(F32)

            def gather_plane(p, carry):
                d, e = p >> 1, p & 1
                for r in range(0, A, 2):
                    at = e * 16 + d * 4 + r if r < 4 else 32 + e * 8 + d * 2
                    pair_of_rows = [gather[u, k, pl.ds(at + i, HALF, stride=ROWS), :] for i in range(2)]
                    tile = jnp.concatenate(pair_of_rows, axis=0).astype(BF16)
                    sendx[u, k, source_plane(base, e, d), r * HALF : r * HALF + 2 * HALF] = tile
                return carry

            lax.fori_loop(0, Z, gather_plane, 0, unroll=True)
            over_planes(sendx.at[u, k], recvx.at[u, k], xs.at[u, k], xr.at[u, k])
        for k in range(2):
            arrived(recvx.at[u, k], xr.at[u, k])
        return gate

    def ending(u, pair, gate, first):
        tri = [recvx[u, k, p].astype(F32) for p in range(Z) for k in range(2)]
        for r in range(pair.shape[0]):
            at = (first + r) * HALF
            tri_row = jnp.concatenate([part[at : at + HALF] for part in tri], axis=0)
            projected = dot(normed(tri_row, 0).astype(BF16), out_ref[u], TN)[:B]
            o_ref[first + r] = pair[r] + gate[r * B : r * B + B] * projected

    loads[1].wait()
    wide_weights(0)
    loads[0].wait()
    zn_a = head_a(0, z_ref[0:4])
    zn_b = head_b(0, zn_a, z_ref[4:6])
    gate_a, gate_b = body(0, (zn_a, zn_b), 0)
    ending(0, z_ref[0:4], gate_a, 0)
    before = len(sent)
    zn_a = head_a(1, o_ref[0:4])
    ending(0, z_ref[4:6], gate_b, 4)
    zn_b = head_b(1, zn_a, o_ref[4:6])
    gate_a, gate_b = body(1, (zn_a, zn_b), before)
    ending(1, o_ref[0:4], gate_a, 0)
    ending(1, o_ref[4:6], gate_b, 4)
    drain(len(sent))


def solution(mesh):
    vmem = pl.BlockSpec(memory_space=pltpu.VMEM)

    def per_device(*operands):
        pair_rep, proj_weights, gate_weights, out_weights = operands
        return pl.pallas_call(
            kernel,
            out_shape=jax.ShapeDtypeStruct(pair_rep.shape, pair_rep.dtype),
            in_specs=[pl.BlockSpec(memory_space=pltpu.HBM)] * 4,
            out_specs=vmem,
            scratch_shapes=[
                pltpu.VMEM(pair_rep.shape, F32),
                pltpu.VMEM(proj_weights.shape, BF16),
                pltpu.VMEM(gate_weights.shape, BF16),
                pltpu.VMEM(out_weights.shape, BF16),
                pltpu.VMEM((2, 2, 4, Z * HALF, C), BF16),
                pltpu.VMEM((2, 2, Z, 2 * HALF, 384), BF16),
                pltpu.VMEM((2, 2, Z, 2 * HALF, 384), BF16),
                pltpu.VMEM((2, Z, 2 * HALF, 256), BF16),
                pltpu.VMEM((2, Z, 2 * HALF, 256), BF16),
                pltpu.VMEM((2, Z, 2 * HALF, 128), BF16),
                pltpu.VMEM((2, Z, 2 * HALF, 128), BF16),
                pltpu.VMEM((2, 2, 2 * HALF * ROWS + 24, 128), F32),
                pltpu.VMEM((2, 2, 2, HALF, 2, 16, 128), BF16),
                pltpu.VMEM((2, 2, 2, HALF, 16, 128), BF16),
                pltpu.VMEM((2, CORES, 2 * CHIPS, 2, 16, 128), BF16),
                pltpu.VMEM((2, CORES, 2 * CHIPS, 16, 128), BF16),
                pltpu.VMEM((2, CHIPS, ROWS, 128), BF16),
                pltpu.VMEM((2, 2, HALF, ROWS, 128), BF16),
                pltpu.VMEM((2, 2, HALF * ROWS + ROWS, 128), F32),
                pltpu.VMEM((2, 2, Z, A * HALF, 128), BF16),
                pltpu.VMEM((2, 2, Z, A * HALF, 128), BF16),
                pltpu.SemaphoreType.DMA((4,)),
                pltpu.SemaphoreType.DMA((2, 4)),
                pltpu.SemaphoreType.DMA((2, 4)),
                pltpu.SemaphoreType.DMA((2, 2)),
                pltpu.SemaphoreType.DMA((2, 2)),
                pltpu.SemaphoreType.DMA((2, 2)),
                pltpu.SemaphoreType.DMA((2, 2)),
                pltpu.SemaphoreType.DMA((2,)),
                pltpu.SemaphoreType.DMA((2, 2)),
                pltpu.SemaphoreType.DMA((2, 2)),
                pltpu.SemaphoreType.DMA((2, 2)),
            ],
            compiler_params=pltpu.CompilerParams(
                collective_id=0, has_side_effects=True, vmem_limit_bytes=48 * 1024 * 1024
            ),
        )(*(pltpu.with_memory_space_constraint(x, pltpu.HBM) for x in operands))

    return jax.shard_map(
        per_device,
        mesh=mesh,
        in_specs=(P("row", "col", None), P(), P(), P()),
        out_specs=P("row", "col", None),
        check_vma=False,
    )
```

```python
import jax
import jax.numpy as jnp
from jax import lax
from jax.experimental import pallas as pl
from jax.experimental.pallas import tpu as pltpu
from jax.sharding import PartitionSpec as P

MESH = pl.DeviceIdType.MESH
F32, BF16 = jnp.float32, jnp.bfloat16
Z, CHIPS, YX, XLO, CORES = 8, 16, 8, 2, 2
A, B, C = 6, 96, 128
HALF = 8
POS = A * B
ROWS = Z * A
FAR_PLANES = (4, 3, 5, 2, 6, 1, 7)
FAR_CHIPS = (10, 11, 9, 14, 6, 8, 2, 15, 13, 7, 5, 12, 4, 3, 1)
PLANE_HOPS = (4, 3, 3, 2, 2, 1, 1)
CHIP_HOPS = (4, 3, 3, 3, 3, 2, 2, 2, 2, 2, 2, 1, 1, 1, 1)
FAR_YX = (5, 7, 3, 4, 1, 6, 2, 0)
NT = (((1,), (1,)), ((), ()))
TN = (((0,), (0,)), ((), ()))


def normed(values, axis):
    centred = values - jnp.mean(values, axis=axis, keepdims=True)
    variance = jnp.mean(centred * centred, axis=axis, keepdims=True)
    return centred * lax.rsqrt(variance + 1e-05)


def dot(a, b, dims=(((1,), (0,)), ((), ()))):
    return lax.dot_general(a, b, dims, preferred_element_type=F32)


def lane_of(rows):
    return lax.broadcasted_iota(jnp.int32, (rows, 128), 1)


def rows_of_a(tiles):
    lane = lane_of(tiles[0].shape[0])
    t0, t1, t2 = tiles
    pieces = [
        t0,
        pltpu.roll(jnp.where(lane < 64, t1, t0), 32, 1),
        pltpu.roll(jnp.where(lane < 32, t2, t1), 64, 1),
        pltpu.roll(t2, 96, 1),
    ]
    return [jnp.where(lane < B, piece, 0.0) for piece in pieces]


def rows_of_b(tile, tail, tail_at):
    lane = lane_of(tile.shape[0])
    fifth = jnp.where(lane < 32, pltpu.roll(tile, 32, 1), pltpu.roll(tail, (32 - tail_at) % 128, 1))
    return [jnp.where(lane < B, piece, 0.0) for piece in (tile, fifth)]


def source_plane(base, e, d):
    return (base + 8 - d + e * (2 * d + 1)) & 7


def row_of(base, z, yx, r):
    delta = (z - base + 8) & 7
    e = jnp.where((delta >= 1) & (delta <= 4), 1, 0)
    d = jnp.where(e == 1, delta - 1, (8 - delta) & 7)
    return jnp.where(r < 4, e * 128 + yx * 16 + d * 4 + r, 256 + e * 64 + yx * 8 + d * 2 + r - 4)


def row_at(base, row):
    in_a, late = row < 256, row - 256
    e = jnp.where(in_a, row // 128, late // 64)
    yx = jnp.where(in_a, row % 128 // 16, late % 64 // 8)
    d = jnp.where(in_a, row % 16 // 4, late % 8 // 2)
    r = jnp.where(in_a, row % 4, 4 + late % 2)
    return source_plane(base, e, d), yx, r


def picks_outgoing(core, base):
    row = lax.broadcasted_iota(jnp.int32, (XLO * 128, YX * ROWS), 0)
    col = lax.broadcasted_iota(jnp.int32, (XLO * 128, YX * ROWS), 1)
    x_lo, jr = row // 128, row % 128
    z, yx, r = 4 * x_lo + 2 * core + jr // 48, jr % 48 // A, jr % A
    return jnp.where((col == row_of(base, z, yx, r)) & (jr < B), 1.0, 0.0).astype(BF16)


def picks_incoming(core, base):
    row = lax.broadcasted_iota(jnp.int32, (YX * ROWS, 4 * 128), 0)
    col = lax.broadcasted_iota(jnp.int32, (YX * ROWS, 4 * 128), 1)
    z, yx, r = row_at(base, row)
    other = jnp.bitwise_xor((z // 2) % 2, core)
    source = (other * 2 + z // 4) * 128 + (z % 2) * 48 + yx * A + r
    return jnp.where(col == source, 1.0, 0.0).astype(BF16)


def reorder(base, base_of_other):
    row = lax.broadcasted_iota(jnp.int32, (YX * ROWS, YX * ROWS), 0)
    col = lax.broadcasted_iota(jnp.int32, (YX * ROWS, YX * ROWS), 1)
    return jnp.where(col == row_of(base_of_other, *row_at(base, row)), 1.0, 0.0).astype(BF16)


def kernel(
    pair_hbm, proj_hbm, gate_hbm, out_hbm, o_ref,
    z_ref, proj_ref, gate_ref, out_ref, wide,
    senda, recva, send2, recv2, send1, recv1, spread, sendpa, sendpb, recvpa, recvpb, sendq, recvq, gather, sendx, recvx, sendy, recvy,
    load, zs, zr, ps, pr, cs, cr, qs, qr, xs, xr,
):
    loads = [
        pltpu.make_async_copy(src, dst, load.at[i])
        for i, (src, dst) in enumerate(
            ((pair_hbm, z_ref), (proj_hbm, proj_ref), (gate_hbm, gate_ref), (out_hbm, out_ref))
        )
    ]
    loads[0].start()
    loads[1].start()
    row, col = lax.axis_index("row"), lax.axis_index("col")
    plane, yx, x_lo, core = row >> 3, row & 7, col >> 1, col & 1
    chip = yx * XLO + x_lo
    chunk_of_chip = x_lo ^ ((yx >> 1) & 1)
    member = (plane + 8 - core) & 1
    base, base_of_other = (plane + 8 - member) & 7, (plane + 7 + member) & 7
    up = 1 - 2 * member
    relays = [((plane + 8 + step * up) & 7, d) for d, step in ((3, -3), (2, 2), (1, -1))]
    planes = [(plane + s) & (Z - 1) for s in FAR_PLANES]
    chips = [chip ^ s for s in FAR_CHIPS]

    def on_plane(other_plane):
        return {"row": other_plane * YX + yx, "col": col}

    def on_chip(other_chip, of_plane=plane):
        return {"row": of_plane * YX + (other_chip >> 1), "col": (other_chip & 1) * CORES + core}

    other_core = {"row": row, "col": col ^ 1}

    barrier = pltpu.get_barrier_semaphore()
    beside = (plane + 8 + up) & 7
    peers = [(hops, on_plane(peer)) for hops, peer in zip(PLANE_HOPS, planes)]
    peers += [(hops, on_chip(peer)) for hops, peer in zip(CHIP_HOPS, chips)]
    peers += [(hops + 1, on_chip(peer, beside)) for hops, peer in zip(CHIP_HOPS, chips)]
    peers = [peer for _, peer in sorted(peers, key=lambda peer: -peer[0])] + [other_core]
    for peer in peers:
        pl.semaphore_signal(barrier, inc=1, device_id=peer, device_id_type=MESH)
    loads[2].start()
    loads[3].start()

    sent = []

    def remote(src, dst, send, recv, peer):
        pltpu.make_async_remote_copy(
            src_ref=src, dst_ref=dst, send_sem=send, recv_sem=recv, device_id=peer, device_id_type=MESH
        ).start()

    def arrived(ref, sem):
        pltpu.make_async_copy(ref, ref, sem).wait()

    def slot_of(some_chip):
        return (some_chip & 1) * YX + (some_chip >> 1)

    def over_planes(src, dst, send, recv):
        for peer in planes:
            remote(src.at[peer], dst.at[plane], send, recv, on_plane(peer))
        pltpu.make_async_copy(src.at[plane], dst.at[plane], recv).start()
        sent.append((src.at[pl.ds(0, Z - 1)], send))

    def to_owners(chunk, src, dst, send, recv):
        here = dst.at[member * CHIPS + slot_of(chip)]

        def owner(m):
            return m * XLO + (chunk ^ ((m >> 1) & 1))

        for s in FAR_YX:
            peer = yx ^ s
            remote(src.at[1 - member, peer], here, send, recv, on_chip(owner(peer), beside))
            if s != 0:
                remote(src.at[member, peer], here, send, recv, on_chip(owner(peer)))
        own = chunk_of_chip == chunk

        @pl.when(own)
        def _():
            pltpu.make_async_copy(src.at[member, yx], here, recv).start()

        @pl.when(jnp.logical_not(own))
        def _():
            remote(src.at[member, yx], here, send, recv, on_chip(chip ^ 1))

    def wide_weights(u):
        for i in range(4):
            turned = proj_ref[u, i].astype(F32).T.reshape(Z, 2, HALF, C)
            for k in range(2):
                wide[u, k, i] = turned[:, k].reshape(Z * HALF, C).astype(BF16)

    def drain(count):
        for _ in range(count):
            arrived(*sent.pop(0))

    def z_parts(u):
        return [
            (senda.at[u, 0], recva.at[u, 0]),
            (send2.at[u], recv2.at[u]),
            (senda.at[u, 1], recva.at[u, 1]),
            (send1.at[u], recv1.at[u]),
        ]

    def issue(u, i):
        src, dst = z_parts(u)[i]
        for relay, d in relays:
            first = (relay + 8 - (member ^ (d & 1))) & 7
            for e in range(2):
                remote(src.at[(first + e) & 7], dst.at[2 * d + e], zs.at[u, i], zr.at[u, i], on_plane(relay))
        for e in range(2):
            pltpu.make_async_copy(src.at[(base + e) & 7], dst.at[e], zr.at[u, i]).start()
        sent.append((src.at[pl.ds(0, 6)], zs.at[u, i]))

    def edges(u, k, zn):
        both = dot(wide[u, k].reshape(4 * Z * HALF, C), zn, NT).reshape(4, Z, HALF, zn.shape[0])
        left = jax.nn.sigmoid(both[0]) * both[1]
        right = jax.nn.sigmoid(both[2]) * both[3]
        return jnp.concatenate([left, right], axis=1).astype(BF16)

    def head_a(u, rows):
        zn = normed(rows.reshape(4 * B, C), -1).astype(BF16)
        senda[u, 0] = edges(u, 0, zn)
        if u == 1:
            issue(u, 0)
        return zn

    def head_b(u, zn_a, rows):
        zn = normed(rows.reshape(2 * B, C), -1).astype(BF16)
        second = edges(u, 1, zn)
        send2[u, :, :, 0:192] = edges(u, 0, zn)
        send2[u, :, :, 192:256] = second[:, :, 128:192]
        send1[u] = second[:, :, 0:128]
        if u == 1:
            issue(u, 1)
        senda[u, 1] = edges(u, 1, zn_a)
        if u == 0:
            pl.semaphore_wait(barrier, len(peers))
            issue(u, 0)
            issue(u, 1)
        issue(u, 2)
        issue(u, 3)
        return zn

    def body(u, zn, before):
        if u == 0:
            wide_weights(1)
            loads[2].wait()
            loads[3].wait()
        gate = [jax.nn.sigmoid(dot(some, gate_ref[u])) for some in zn]
        picks = picks_outgoing(core, base) if u == 0 else picks_incoming(core, base)
        other_picks = picks_outgoing(core, base_of_other) if u == 0 else None
        in_order = reorder(base, base_of_other)
        drain(before)

        for k in range(2):
            for part in range(2):
                arrived(z_parts(u)[2 * k + part][1], zr.at[u, 2 * k + part])

                def spread_plane(p, carry):
                    if part == 0:
                        tiles = [recva[u, k, p, :, t * 128 : t * 128 + 128].astype(F32) for t in range(3)]
                        pieces = rows_of_a(tiles)
                    else:
                        tile = recv2[u, p, :, 0:128] if k == 0 else recv1[u, p]
                        pieces = rows_of_b(tile.astype(F32), recv2[u, p, :, 128:256].astype(F32), 64 * k)
                    d, e = p >> 1, p & 1
                    for i, piece in enumerate(pieces):
                        at = e * 2 * HALF * 24 + (d * 4 + i if part == 0 else 16 + d * 2 + i)
                        spread[u, k, pl.ds(at, 2 * HALF, stride=24), :] = piece
                    return carry

                lax.fori_loop(0, Z, spread_plane, 0, unroll=True)
                for e in range(2):
                    for m in range(HALF):
                        at = [(e * 2 * HALF + side * HALF + m) * 24 for side in range(2)]
                        if part == 0:
                            for side in range(2):
                                sendpa[u, k, e, m, side] = spread[u, k, at[side] : at[side] + 16, :].astype(BF16)
                        else:
                            both = [spread[u, k, at[side] + 16 : at[side] + 24, :] for side in range(2)]
                            sendpb[u, k, e, m] = jnp.concatenate(both, axis=0).astype(BF16)
                sendp, recvp = ((sendpa, recvpa), (sendpb, recvpb))[part]
                to_owners(k, sendp.at[u, k], recvp.at[u, 0], ps.at[u, part], pr.at[u, part])

        def shared(part, c):
            if u == 1 and part == 0:
                return recvpa.at[u, c, :, 0]
            return (recvpa, recvpb)[part].at[u, c]

        for part, recvp in enumerate((recvpa, recvpb)):
            sent.append((recvp.at[u, 0, pl.ds(0, 2 * CHIPS - 1)], ps.at[u, part]))
            arrived(recvp.at[u, 0], pr.at[u, part])
            remote(shared(part, 0), shared(part, 1), cs.at[u, part], cr.at[u, part], other_core)
            sent.append((shared(part, 0), cs.at[u, part]))

        def block_of(part, side, c, x):
            rows = []
            for e in range(2):
                slots = pl.ds(e * CHIPS + x * YX, YX)
                if part == 0:
                    rows.append(recvpa[u, c, slots, side].reshape(128, 128))
                else:
                    both = recvpb[u, c, slots].astype(F32)
                    rows.append(both[:, side * 8 : side * 8 + 8].reshape(64, 128).astype(BF16))
            return jnp.concatenate(rows, axis=0)

        def blocks(part, side, c):
            return jnp.concatenate([block_of(part, side, c, x) for x in range(XLO)], axis=1)

        halves, lefts = [], []
        for part in range(2):
            arrived(shared(part, 1), cr.at[u, part])
            here = slice(256 * part, 256 + 128 * part)
            left_of_other = dot(in_order[here, here], blocks(part, 0, 1)).astype(BF16)
            left = jnp.concatenate([blocks(part, 0, 0), left_of_other], axis=1)
            if u == 0:
                right = [dot(which[:, here], blocks(part, 1, c)) for c, which in enumerate((picks, other_picks))]
                halves.append(jnp.concatenate(right, axis=1))
                lefts.append(left)
            else:
                halves.append(dot(dot(picks, left, NT).astype(BF16), blocks(part, 1, 0)))
        tri = halves[0] + halves[1]
        if u == 0:
            tri = dot(jnp.concatenate(lefts, axis=0), tri.astype(BF16), NT)
        for x in range(XLO):
            block = tri[:, x * 128 : x * 128 + 128]
            slots = pl.ds(x * YX, YX)
            for e in range(2):
                part_a = block[e * 128 : e * 128 + 128].astype(BF16)
                sendq[u, slots, e * 16 : e * 16 + 16] = part_a.reshape(YX, 16, 128)
            part_b = block[256:384].reshape(2, YX, 8, 128)
            sendq[u, slots, 32:48] = jnp.concatenate([part_b[0], part_b[1]], axis=1).astype(BF16)
        here = recvq.at[u, chunk_of_chip, yx]
        for peer in chips:
            remote(sendq.at[u, slot_of(peer)], here, qs.at[u], qr.at[u, chunk_of_chip], on_chip(peer))
        pltpu.make_async_copy(sendq.at[u, slot_of(chip)], here, qr.at[u, chunk_of_chip]).start()
        sent.append((sendq.at[u, pl.ds(0, CHIPS - 1)], qs.at[u]))

        if u == 1:
            drain(len(sent))
        for k in range(2):
            arrived(recvq.at[u, k], qr.at[u, k])
            gather[u, k, 0 : HALF * ROWS] = recvq[u, k].reshape(HALF * ROWS, 128).astype(F32)

            def gather_plane(p, carry):
                d, e = p >> 1, p & 1
                lane = lane_of(2 * HALF)
                threes = []
                for i in range(3):
                    rows = []
                    for r in (i, 3 + i):
                        at = e * 16 + d * 4 + r if r < 4 else 32 + e * 8 + d * 2 + r - 4
                        rows.append(gather[u, k, pl.ds(at, HALF, stride=ROWS), :])
                    threes.append(jnp.concatenate(rows, axis=0))
                t0, t1, t2 = threes[0], pltpu.roll(threes[1], 96, 1), pltpu.roll(threes[2], 64, 1)
                to = source_plane(base, e, d)
                tiles = [jnp.where(lane < 96, t0, t1), jnp.where(lane < 64, t1, t2)]
                for t, tile in enumerate(tiles):
                    (sendx, sendy)[k][u, to, :, t * 128 : t * 128 + 128] = tile.astype(BF16)
                if k == 0:
                    sendy[u, to, :, 256:384] = pltpu.roll(t2, 32, 1).astype(BF16)
                else:
                    kept = sendy[u, to, :, 256:384].astype(F32)
                    sendy[u, to, :, 256:384] = jnp.where(lane < 32, t2, kept).astype(BF16)
                return carry

            lax.fori_loop(0, Z, gather_plane, 0, unroll=True)
            over_planes((sendx, sendy)[k].at[u], (recvx, recvy)[k].at[u], xs.at[u, k], xr.at[u, k])
        for k in range(2):
            arrived((recvx, recvy)[k].at[u], xr.at[u, k])
        return gate

    def ending(u, pair, gate):
        gate = jnp.concatenate(gate, axis=0)
        for h in range(2):
            parts = []
            for p in range(Z):
                first = recvx[u, p].astype(F32)[h * HALF : h * HALF + HALF]
                second = recvy[u, p].astype(F32)[h * HALF : h * HALF + HALF]
                parts.append(jnp.concatenate([first, pltpu.roll(second[:, 256:384], 96, 1)], axis=1))
                parts.append(second)
            tri = jnp.concatenate(parts, axis=0)
            projected = dot(normed(tri, 0).astype(BF16), out_ref[u], TN)[: 3 * B]
            here = slice(h * 3 * B, h * 3 * B + 3 * B)
            o_ref[3 * h : 3 * h + 3] = pair[3 * h : 3 * h + 3] + (gate[here] * projected).reshape(3, B, C)

    loads[1].wait()
    wide_weights(0)
    loads[0].wait()
    zn_a = head_a(0, z_ref[0:4])
    zn_b = head_b(0, zn_a, z_ref[4:6])
    gate_a, gate_b = body(0, (zn_a, zn_b), 0)
    ending(0, z_ref, (gate_a, gate_b))
    before = len(sent)
    zn_a = head_a(1, o_ref[0:4])
    zn_b = head_b(1, zn_a, o_ref[4:6])
    gate_a, gate_b = body(1, (zn_a, zn_b), before)
    ending(1, o_ref, (gate_a, gate_b))
    drain(len(sent))


def solution(mesh):
    vmem = pl.BlockSpec(memory_space=pltpu.VMEM)

    def per_device(*operands):
        pair_rep, proj_weights, gate_weights, out_weights = operands
        return pl.pallas_call(
            kernel,
            out_shape=jax.ShapeDtypeStruct(pair_rep.shape, pair_rep.dtype),
            in_specs=[pl.BlockSpec(memory_space=pltpu.HBM)] * 4,
            out_specs=vmem,
            scratch_shapes=[
                pltpu.VMEM(pair_rep.shape, F32),
                pltpu.VMEM(proj_weights.shape, BF16),
                pltpu.VMEM(gate_weights.shape, BF16),
                pltpu.VMEM(out_weights.shape, BF16),
                pltpu.VMEM((2, 2, 4, Z * HALF, C), BF16),
                pltpu.VMEM((2, 2, Z, 2 * HALF, 384), BF16),
                pltpu.VMEM((2, 2, Z, 2 * HALF, 384), BF16),
                pltpu.VMEM((2, Z, 2 * HALF, 256), BF16),
                pltpu.VMEM((2, Z, 2 * HALF, 256), BF16),
                pltpu.VMEM((2, Z, 2 * HALF, 128), BF16),
                pltpu.VMEM((2, Z, 2 * HALF, 128), BF16),
                pltpu.VMEM((2, 2, 2 * HALF * ROWS + 24, 128), F32),
                pltpu.VMEM((2, 2, 2, HALF, 2, 16, 128), BF16),
                pltpu.VMEM((2, 2, 2, HALF, 16, 128), BF16),
                pltpu.VMEM((2, CORES, 2 * CHIPS, 2, 16, 128), BF16),
                pltpu.VMEM((2, CORES, 2 * CHIPS, 16, 128), BF16),
                pltpu.VMEM((2, CHIPS, ROWS, 128), BF16),
                pltpu.VMEM((2, 2, HALF, ROWS, 128), BF16),
                pltpu.VMEM((2, 2, HALF * ROWS + ROWS, 128), F32),
                pltpu.VMEM((2, Z, 2 * HALF, 256), BF16),
                pltpu.VMEM((2, Z, 2 * HALF, 256), BF16),
                pltpu.VMEM((2, Z, 2 * HALF, 384), BF16),
                pltpu.VMEM((2, Z, 2 * HALF, 384), BF16),
                pltpu.SemaphoreType.DMA((4,)),
                pltpu.SemaphoreType.DMA((2, 4)),
                pltpu.SemaphoreType.DMA((2, 4)),
                pltpu.SemaphoreType.DMA((2, 2)),
                pltpu.SemaphoreType.DMA((2, 2)),
                pltpu.SemaphoreType.DMA((2, 2)),
                pltpu.SemaphoreType.DMA((2, 2)),
                pltpu.SemaphoreType.DMA((2,)),
                pltpu.SemaphoreType.DMA((2, 2)),
                pltpu.SemaphoreType.DMA((2, 2)),
                pltpu.SemaphoreType.DMA((2, 2)),
            ],
            compiler_params=pltpu.CompilerParams(
                collective_id=0, has_side_effects=True, vmem_limit_bytes=48 * 1024 * 1024
            ),
        )(*(pltpu.with_memory_space_constraint(x, pltpu.HBM) for x in operands))

    return jax.shard_map(
        per_device,
        mesh=mesh,
        in_specs=(P("row", "col", None), P(), P(), P()),
        out_specs=P("row", "col", None),
        check_vma=False,
    )
```

```python
import jax
import jax.numpy as jnp
from jax import lax
from jax.experimental import pallas as pl
from jax.experimental.pallas import tpu as pltpu
from jax.sharding import PartitionSpec as P

MESH = pl.DeviceIdType.MESH
F32, BF16 = jnp.float32, jnp.bfloat16
Z, CHIPS, YX, XLO, CORES = 8, 16, 8, 2, 2
A, B, C = 6, 96, 128
HALF = 8
POS = A * B
ROWS = Z * A
FAR_PLANES = (4, 3, 5, 2, 6, 1, 7)
FAR_CHIPS = (10, 11, 9, 14, 6, 8, 2, 15, 13, 7, 5, 12, 4, 3, 1)
PLANE_HOPS = (4, 3, 3, 2, 2, 1, 1)
CHIP_HOPS = (4, 3, 3, 3, 3, 2, 2, 2, 2, 2, 2, 1, 1, 1, 1)
FAR_YX = (5, 7, 3, 4, 1, 6, 2, 0)
NT = (((1,), (1,)), ((), ()))
TN = (((0,), (0,)), ((), ()))


def normed(values, axis):
    centred = values - jnp.mean(values, axis=axis, keepdims=True)
    variance = jnp.mean(centred * centred, axis=axis, keepdims=True)
    return centred * lax.rsqrt(variance + 1e-05)


def dot(a, b, dims=(((1,), (0,)), ((), ()))):
    return lax.dot_general(a, b, dims, preferred_element_type=F32)


def lane_of(rows):
    return lax.broadcasted_iota(jnp.int32, (rows, 128), 1)


def rows_of_a(tiles):
    lane = lane_of(tiles[0].shape[0])
    t0, t1, t2 = tiles
    pieces = [
        t0,
        pltpu.roll(jnp.where(lane < 64, t1, t0), 32, 1),
        pltpu.roll(jnp.where(lane < 32, t2, t1), 64, 1),
        pltpu.roll(t2, 96, 1),
    ]
    return [jnp.where(lane < B, piece, 0.0) for piece in pieces]


def rows_of_b(tile, tail, tail_at):
    lane = lane_of(tile.shape[0])
    fifth = jnp.where(lane < 32, pltpu.roll(tile, 32, 1), pltpu.roll(tail, (32 - tail_at) % 128, 1))
    return [jnp.where(lane < B, piece, 0.0) for piece in (tile, fifth)]


def source_plane(base, e, d):
    return (base + 8 - d + e * (2 * d + 1)) & 7


def row_of(base, z, yx, r):
    delta = (z - base + 8) & 7
    e = jnp.where((delta >= 1) & (delta <= 4), 1, 0)
    d = jnp.where(e == 1, delta - 1, (8 - delta) & 7)
    return jnp.where(r < 4, e * 128 + yx * 16 + d * 4 + r, 256 + e * 64 + yx * 8 + d * 2 + r - 4)


def row_at(base, row):
    in_a, late = row < 256, row - 256
    e = jnp.where(in_a, row // 128, late // 64)
    yx = jnp.where(in_a, row % 128 // 16, late % 64 // 8)
    d = jnp.where(in_a, row % 16 // 4, late % 8 // 2)
    r = jnp.where(in_a, row % 4, 4 + late % 2)
    return source_plane(base, e, d), yx, r


def picks_outgoing(core, base):
    row = lax.broadcasted_iota(jnp.int32, (XLO * 128, YX * ROWS), 0)
    col = lax.broadcasted_iota(jnp.int32, (XLO * 128, YX * ROWS), 1)
    x_lo, jr = row // 128, row % 128
    z, yx, r = 4 * x_lo + 2 * core + jr // 48, jr % 48 // A, jr % A
    return jnp.where((col == row_of(base, z, yx, r)) & (jr < B), 1.0, 0.0).astype(BF16)


def picks_incoming(core, base):
    row = lax.broadcasted_iota(jnp.int32, (YX * ROWS, 4 * 128), 0)
    col = lax.broadcasted_iota(jnp.int32, (YX * ROWS, 4 * 128), 1)
    z, yx, r = row_at(base, row)
    other = jnp.bitwise_xor((z // 2) % 2, core)
    source = (other * 2 + z // 4) * 128 + (z % 2) * 48 + yx * A + r
    return jnp.where(col == source, 1.0, 0.0).astype(BF16)


def reorder(base, base_of_other):
    row = lax.broadcasted_iota(jnp.int32, (YX * ROWS, YX * ROWS), 0)
    col = lax.broadcasted_iota(jnp.int32, (YX * ROWS, YX * ROWS), 1)
    return jnp.where(col == row_of(base_of_other, *row_at(base, row)), 1.0, 0.0).astype(BF16)


def kernel(
    pair_hbm, proj_hbm, gate_hbm, out_hbm, o_ref,
    z_ref, proj_ref, gate_ref, out_ref, wide,
    senda, recva, send2, recv2, send1, recv1, spread, sendpa, sendpb, recvpa, recvpb, sendq, recvq, gather, sendx, recvx, sendy, recvy,
    load, zs, zr, ps, pr, cs, cr, qs, qr, xs, xr,
):
    loads = [
        pltpu.make_async_copy(src, dst, load.at[i])
        for i, (src, dst) in enumerate(
            ((pair_hbm, z_ref), (proj_hbm, proj_ref), (gate_hbm, gate_ref), (out_hbm, out_ref))
        )
    ]
    loads[0].start()
    loads[1].start()
    row, col = lax.axis_index("row"), lax.axis_index("col")
    plane, yx, x_lo, core = row >> 3, row & 7, col >> 1, col & 1
    chip = yx * XLO + x_lo
    chunk_of_chip = x_lo ^ ((yx >> 1) & 1)
    member = (plane + 8 - core) & 1
    base, base_of_other = (plane + 8 - member) & 7, (plane + 7 + member) & 7
    up = 1 - 2 * member
    relays = [((plane + 8 + step * up) & 7, d) for d, step in ((3, -3), (2, 2), (1, -1))]
    planes = [(plane + s) & (Z - 1) for s in FAR_PLANES]
    chips = [chip ^ s for s in FAR_CHIPS]

    def on_plane(other_plane):
        return {"row": other_plane * YX + yx, "col": col}

    def on_chip(other_chip, of_plane=plane):
        return {"row": of_plane * YX + (other_chip >> 1), "col": (other_chip & 1) * CORES + core}

    other_core = {"row": row, "col": col ^ 1}

    barrier = pltpu.get_barrier_semaphore()
    beside = (plane + 8 + up) & 7
    peers = [(hops, on_plane(peer)) for hops, peer in zip(PLANE_HOPS, planes)]
    peers += [(hops, on_chip(peer)) for hops, peer in zip(CHIP_HOPS, chips)]
    peers += [(hops + 1, on_chip(peer, beside)) for hops, peer in zip(CHIP_HOPS, chips)]
    peers = [peer for _, peer in sorted(peers, key=lambda peer: -peer[0])] + [other_core]
    for peer in peers:
        pl.semaphore_signal(barrier, inc=1, device_id=peer, device_id_type=MESH)
    loads[2].start()
    loads[3].start()

    sent = []

    def remote(src, dst, send, recv, peer):
        pltpu.make_async_remote_copy(
            src_ref=src, dst_ref=dst, send_sem=send, recv_sem=recv, device_id=peer, device_id_type=MESH
        ).start()

    def arrived(ref, sem):
        pltpu.make_async_copy(ref, ref, sem).wait()

    def slot_of(some_chip):
        return (some_chip & 1) * YX + (some_chip >> 1)

    def over_planes(src, dst, send, recv):
        for peer in planes:
            remote(src.at[peer], dst.at[plane], send, recv, on_plane(peer))
        pltpu.make_async_copy(src.at[plane], dst.at[plane], recv).start()
        sent.append((src.at[pl.ds(0, Z - 1)], send))

    def to_owners(chunk, src, dst, send, recv):
        here = dst.at[member * CHIPS + slot_of(chip)]

        def owner(m):
            return m * XLO + (chunk ^ ((m >> 1) & 1))

        for s in FAR_YX:
            peer = yx ^ s
            remote(src.at[1 - member, peer], here, send, recv, on_chip(owner(peer), beside))
            if s != 0:
                remote(src.at[member, peer], here, send, recv, on_chip(owner(peer)))
        own = chunk_of_chip == chunk

        @pl.when(own)
        def _():
            pltpu.make_async_copy(src.at[member, yx], here, recv).start()

        @pl.when(jnp.logical_not(own))
        def _():
            remote(src.at[member, yx], here, send, recv, on_chip(chip ^ 1))

    def wide_weights(u):
        for i in range(4):
            turned = proj_ref[u, i].astype(F32).T.reshape(Z, 2, HALF, C)
            for k in range(2):
                wide[u, k, i] = turned[:, k].reshape(Z * HALF, C).astype(BF16)

    def drain(count):
        for _ in range(count):
            arrived(*sent.pop(0))

    def z_parts(u):
        return [
            (senda.at[u, 0], recva.at[u, 0]),
            (send2.at[u], recv2.at[u]),
            (senda.at[u, 1], recva.at[u, 1]),
            (send1.at[u], recv1.at[u]),
        ]

    def issue(u, i, lanes=None, last=True):
        src, dst = z_parts(u)[i]
        if lanes is not None:
            src, dst = src.at[:, :, lanes], dst.at[:, :, lanes]
        for relay, d in relays:
            first = (relay + 8 - (member ^ (d & 1))) & 7
            for e in range(2):
                remote(src.at[(first + e) & 7], dst.at[2 * d + e], zs.at[u, i], zr.at[u, i], on_plane(relay))
        for e in range(2):
            pltpu.make_async_copy(src.at[(base + e) & 7], dst.at[e], zr.at[u, i]).start()
        if last:
            sent.append((z_parts(u)[i][0].at[pl.ds(0, 6)], zs.at[u, i]))

    def edges(u, k, zn):
        both = dot(wide[u, k].reshape(4 * Z * HALF, C), zn, NT).reshape(4, Z, HALF, zn.shape[0])
        left = jax.nn.sigmoid(both[0]) * both[1]
        right = jax.nn.sigmoid(both[2]) * both[3]
        return jnp.concatenate([left, right], axis=1).astype(BF16)

    def head_a(u, rows):
        zn = normed(rows.reshape(4 * B, C), -1).astype(BF16)
        senda[u, 0] = edges(u, 0, zn)
        if u == 1:
            issue(u, 0)
        return zn

    def head_b(u, zn_a, rows):
        zn = normed(rows.reshape(2 * B, C), -1).astype(BF16)
        second = edges(u, 1, zn)
        send2[u, :, :, 0:192] = edges(u, 0, zn)
        send2[u, :, :, 192:256] = second[:, :, 128:192]
        send1[u] = second[:, :, 0:128]
        if u == 1:
            issue(u, 1)
        senda[u, 1] = edges(u, 1, zn_a)
        if u == 0:
            pl.semaphore_wait(barrier, len(peers))
            issue(u, 0)
            issue(u, 1)
        issue(u, 2)
        issue(u, 3)
        return zn

    def body(u, zn, before):
        if u == 0:
            wide_weights(1)
            loads[2].wait()
            loads[3].wait()
        gate = [jax.nn.sigmoid(dot(some, gate_ref[u])) for some in zn]
        picks = picks_outgoing(core, base) if u == 0 else picks_incoming(core, base)
        other_picks = picks_outgoing(core, base_of_other) if u == 0 else None
        in_order = reorder(base, base_of_other)
        drain(before)

        for k in range(2):
            for part in range(2):
                arrived(z_parts(u)[2 * k + part][1], zr.at[u, 2 * k + part])

                def spread_plane(p, carry):
                    if part == 0:
                        tiles = [recva[u, k, p, :, t * 128 : t * 128 + 128].astype(F32) for t in range(3)]
                        pieces = rows_of_a(tiles)
                    else:
                        tile = recv2[u, p, :, 0:128] if k == 0 else recv1[u, p]
                        pieces = rows_of_b(tile.astype(F32), recv2[u, p, :, 128:256].astype(F32), 64 * k)
                    d, e = p >> 1, p & 1
                    for i, piece in enumerate(pieces):
                        at = e * 2 * HALF * 24 + (d * 4 + i if part == 0 else 16 + d * 2 + i)
                        spread[u, k, pl.ds(at, 2 * HALF, stride=24), :] = piece
                    return carry

                lax.fori_loop(0, Z, spread_plane, 0, unroll=True)
                for e in range(2):
                    for m in range(HALF):
                        at = [(e * 2 * HALF + side * HALF + m) * 24 for side in range(2)]
                        if part == 0:
                            for side in range(2):
                                sendpa[u, k, e, m, side] = spread[u, k, at[side] : at[side] + 16, :].astype(BF16)
                        else:
                            both = [spread[u, k, at[side] + 16 : at[side] + 24, :] for side in range(2)]
                            sendpb[u, k, e, m] = jnp.concatenate(both, axis=0).astype(BF16)
                sendp, recvp = ((sendpa, recvpa), (sendpb, recvpb))[part]
                to_owners(k, sendp.at[u, k], recvp.at[u, 0], ps.at[u, part], pr.at[u, part])

        def shared(part, c):
            if u == 1 and part == 0:
                return recvpa.at[u, c, :, 0]
            return (recvpa, recvpb)[part].at[u, c]

        for part, recvp in enumerate((recvpa, recvpb)):
            sent.append((recvp.at[u, 0, pl.ds(0, 2 * CHIPS - 1)], ps.at[u, part]))
            arrived(recvp.at[u, 0], pr.at[u, part])
            remote(shared(part, 0), shared(part, 1), cs.at[u, part], cr.at[u, part], other_core)
            sent.append((shared(part, 0), cs.at[u, part]))

        def block_of(part, side, c, x):
            rows = []
            for e in range(2):
                slots = pl.ds(e * CHIPS + x * YX, YX)
                if part == 0:
                    rows.append(recvpa[u, c, slots, side].reshape(128, 128))
                else:
                    both = recvpb[u, c, slots].astype(F32)
                    rows.append(both[:, side * 8 : side * 8 + 8].reshape(64, 128).astype(BF16))
            return jnp.concatenate(rows, axis=0)

        def blocks(part, side, c):
            return jnp.concatenate([block_of(part, side, c, x) for x in range(XLO)], axis=1)

        halves, lefts = [], []
        for part in range(2):
            arrived(shared(part, 1), cr.at[u, part])
            here = slice(256 * part, 256 + 128 * part)
            left_of_other = dot(in_order[here, here], blocks(part, 0, 1)).astype(BF16)
            left = jnp.concatenate([blocks(part, 0, 0), left_of_other], axis=1)
            if u == 0:
                right = [dot(which[:, here], blocks(part, 1, c)) for c, which in enumerate((picks, other_picks))]
                halves.append(jnp.concatenate(right, axis=1))
                lefts.append(left)
            else:
                halves.append(dot(dot(picks, left, NT).astype(BF16), blocks(part, 1, 0)))
        tri = halves[0] + halves[1]
        if u == 0:
            tri = dot(jnp.concatenate(lefts, axis=0), tri.astype(BF16), NT)
        for x in range(XLO):
            block = tri[:, x * 128 : x * 128 + 128]
            slots = pl.ds(x * YX, YX)
            for e in range(2):
                part_a = block[e * 128 : e * 128 + 128].astype(BF16)
                sendq[u, slots, e * 16 : e * 16 + 16] = part_a.reshape(YX, 16, 128)
            part_b = block[256:384].reshape(2, YX, 8, 128)
            sendq[u, slots, 32:48] = jnp.concatenate([part_b[0], part_b[1]], axis=1).astype(BF16)
        here = recvq.at[u, chunk_of_chip, yx]
        for peer in chips:
            remote(sendq.at[u, slot_of(peer)], here, qs.at[u], qr.at[u, chunk_of_chip], on_chip(peer))
        pltpu.make_async_copy(sendq.at[u, slot_of(chip)], here, qr.at[u, chunk_of_chip]).start()
        sent.append((sendq.at[u, pl.ds(0, CHIPS - 1)], qs.at[u]))

        if u == 1:
            drain(len(sent))
        for k in range(2):
            arrived(recvq.at[u, k], qr.at[u, k])
            gather[u, k, 0 : HALF * ROWS] = recvq[u, k].reshape(HALF * ROWS, 128).astype(F32)

            def gather_plane(p, carry):
                d, e = p >> 1, p & 1
                lane = lane_of(2 * HALF)
                threes = []
                for i in range(3):
                    rows = []
                    for r in (i, 3 + i):
                        at = e * 16 + d * 4 + r if r < 4 else 32 + e * 8 + d * 2 + r - 4
                        rows.append(gather[u, k, pl.ds(at, HALF, stride=ROWS), :])
                    threes.append(jnp.concatenate(rows, axis=0))
                t0, t1, t2 = threes[0], pltpu.roll(threes[1], 96, 1), pltpu.roll(threes[2], 64, 1)
                to = source_plane(base, e, d)
                tiles = [jnp.where(lane < 96, t0, t1), jnp.where(lane < 64, t1, t2)]
                for t, tile in enumerate(tiles):
                    (sendx, sendy)[k][u, to, :, t * 128 : t * 128 + 128] = tile.astype(BF16)
                if k == 0:
                    sendy[u, to, :, 256:384] = pltpu.roll(t2, 32, 1).astype(BF16)
                else:
                    kept = sendy[u, to, :, 256:384].astype(F32)
                    sendy[u, to, :, 256:384] = jnp.where(lane < 32, t2, kept).astype(BF16)
                return carry

            lax.fori_loop(0, Z, gather_plane, 0, unroll=True)
            over_planes((sendx, sendy)[k].at[u], (recvx, recvy)[k].at[u], xs.at[u, k], xr.at[u, k])
        for k in range(2):
            arrived((recvx, recvy)[k].at[u], xr.at[u, k])
        return gate

    def ending(u, pair, gate, halves=(0, 1)):
        gate = jnp.concatenate(gate, axis=0)
        for h in halves:
            parts = []
            for p in range(Z):
                first = recvx[u, p].astype(F32)[h * HALF : h * HALF + HALF]
                second = recvy[u, p].astype(F32)[h * HALF : h * HALF + HALF]
                parts.append(jnp.concatenate([first, pltpu.roll(second[:, 256:384], 96, 1)], axis=1))
                parts.append(second)
            tri = jnp.concatenate(parts, axis=0)
            projected = dot(normed(tri, 0).astype(BF16), out_ref[u], TN)[: 3 * B]
            here = slice(h * 3 * B, h * 3 * B + 3 * B)
            o_ref[3 * h : 3 * h + 3] = pair[3 * h : 3 * h + 3] + (gate[here] * projected).reshape(3, B, C)

    loads[1].wait()
    wide_weights(0)
    loads[0].wait()
    zn_a = head_a(0, z_ref[0:4])
    zn_b = head_b(0, zn_a, z_ref[4:6])
    gate_a, gate_b = body(0, (zn_a, zn_b), 0)
    ending(0, z_ref, (gate_a, gate_b), (0,))
    before = len(sent)
    zn = normed(o_ref[0:3].reshape(3 * B, C), -1).astype(BF16)
    senda[1, 0, :, :, 0:256] = edges(1, 0, zn[0:256])
    issue(1, 0, pl.ds(0, 256), False)
    ending(0, z_ref, (gate_a, gate_b), (1,))
    late = normed(o_ref[3].reshape(B, C), -1).astype(BF16)
    zn_a = jnp.concatenate([zn, late], axis=0)
    senda[1, 0, :, :, 256:384] = edges(1, 0, zn_a[256:384])
    issue(1, 0, pl.ds(256, 128))
    zn_b = head_b(1, zn_a, o_ref[4:6])
    gate_a, gate_b = body(1, (zn_a, zn_b), before)
    ending(1, o_ref, (gate_a, gate_b))
    drain(len(sent))


def solution(mesh):
    vmem = pl.BlockSpec(memory_space=pltpu.VMEM)

    def per_device(*operands):
        pair_rep, proj_weights, gate_weights, out_weights = operands
        return pl.pallas_call(
            kernel,
            out_shape=jax.ShapeDtypeStruct(pair_rep.shape, pair_rep.dtype),
            in_specs=[pl.BlockSpec(memory_space=pltpu.HBM)] * 4,
            out_specs=vmem,
            scratch_shapes=[
                pltpu.VMEM(pair_rep.shape, F32),
                pltpu.VMEM(proj_weights.shape, BF16),
                pltpu.VMEM(gate_weights.shape, BF16),
                pltpu.VMEM(out_weights.shape, BF16),
                pltpu.VMEM((2, 2, 4, Z * HALF, C), BF16),
                pltpu.VMEM((2, 2, Z, 2 * HALF, 384), BF16),
                pltpu.VMEM((2, 2, Z, 2 * HALF, 384), BF16),
                pltpu.VMEM((2, Z, 2 * HALF, 256), BF16),
                pltpu.VMEM((2, Z, 2 * HALF, 256), BF16),
                pltpu.VMEM((2, Z, 2 * HALF, 128), BF16),
                pltpu.VMEM((2, Z, 2 * HALF, 128), BF16),
                pltpu.VMEM((2, 2, 2 * HALF * ROWS + 24, 128), F32),
                pltpu.VMEM((2, 2, 2, HALF, 2, 16, 128), BF16),
                pltpu.VMEM((2, 2, 2, HALF, 16, 128), BF16),
                pltpu.VMEM((2, CORES, 2 * CHIPS, 2, 16, 128), BF16),
                pltpu.VMEM((2, CORES, 2 * CHIPS, 16, 128), BF16),
                pltpu.VMEM((2, CHIPS, ROWS, 128), BF16),
                pltpu.VMEM((2, 2, HALF, ROWS, 128), BF16),
                pltpu.VMEM((2, 2, HALF * ROWS + ROWS, 128), F32),
                pltpu.VMEM((2, Z, 2 * HALF, 256), BF16),
                pltpu.VMEM((2, Z, 2 * HALF, 256), BF16),
                pltpu.VMEM((2, Z, 2 * HALF, 384), BF16),
                pltpu.VMEM((2, Z, 2 * HALF, 384), BF16),
                pltpu.SemaphoreType.DMA((4,)),
                pltpu.SemaphoreType.DMA((2, 4)),
                pltpu.SemaphoreType.DMA((2, 4)),
                pltpu.SemaphoreType.DMA((2, 2)),
                pltpu.SemaphoreType.DMA((2, 2)),
                pltpu.SemaphoreType.DMA((2, 2)),
                pltpu.SemaphoreType.DMA((2, 2)),
                pltpu.SemaphoreType.DMA((2,)),
                pltpu.SemaphoreType.DMA((2, 2)),
                pltpu.SemaphoreType.DMA((2, 2)),
                pltpu.SemaphoreType.DMA((2, 2)),
            ],
            compiler_params=pltpu.CompilerParams(
                collective_id=0, has_side_effects=True, vmem_limit_bytes=48 * 1024 * 1024
            ),
        )(*(pltpu.with_memory_space_constraint(x, pltpu.HBM) for x in operands))

    return jax.shard_map(
        per_device,
        mesh=mesh,
        in_specs=(P("row", "col", None), P(), P(), P()),
        out_specs=P("row", "col", None),
        check_vma=False,
    )
```
